32 devices in a mesh: outer: 8 (over y, x, core), inner: 4 (over z).
Axes of the slice: x: 2, y: 2, z: 4, core: 2. Of those that a mesh axis runs over, the one named last changes fastest.
Arguments:
- queries: bfloat16 [4096, 5120], P(('outer', 'inner')), may hold values from -100 to 100
- key_values: bfloat16 [4096, 2048], P(('outer', 'inner')), may hold values from -64 to 64
- doc_lengths: int32 [8, 8], P('outer'), may hold values from 1 to 256, 512 in all within a row
- pairing: int32 [8], replicated, may hold values from 0 to 7, as said below
- swap_ids: int32 [8, 4, 2], P('outer', 'inner'), may hold values from 0 to 3, as said below
- dest: int32 [4096, 1], P(('outer', 'inner')), may hold values from 0 to 3; in each aligned block of 128 rows (0 to 127, 128 to 255, ...) at most 64 rows name the same one
- gain: float32 [5120], replicated, may hold values from 0.1 to 1.9
Outputs:
- normed: bfloat16 [8192, 5120], P(('outer', 'inner'))
The draws below stay inside these ranges and needn't reach their ends.
Inputs may be any that keep to these rules, and one draw needn't show every extreme that they name: pairing[g] = g XOR m for one m of 1 to 7 in each draw, so pairing[pairing[g]] = g. Each device's listed numbers are distinct and increasing, and swap_ids[pairing[g]] = swap_ids[g]. `dest`: the rows of one device name each destination at most 64 times.
All inputs are finite; a program needn't handle non-finite values.
Results may differ from the reference program's by a relative error of at most 0.0059.
Values may be sent and summed in bfloat16 or wider, within the bound.
No kernel may reach another device: no remote copies, remote signals or barrier semaphores. Data moves between devices by JAX's collectives and lax.ppermute only.
A program may use at most 128 MiB of HBM per device.

```python
import math
import jax
import jax.numpy as jnp
import numpy as np
from jax import lax

QUERY_HEADS = 40
KEY_VALUE_HEADS = 8
HEAD_SIZE = 128
TOK_DEV = 128
BLK = 32
NSWAP = 2
NDOCS = 8
GROUP = 512
CAP = 64
TOKEN_TOTAL = 4096
N_OUTER = 8
N_INNER = 4


def pair_mask(key):
    return jax.random.randint(jax.random.fold_in(key, 11), (), 1, N_OUTER, dtype=jnp.int32)


def draw_pairing(key, part):
    mask_bits = pair_mask(key)
    return jnp.bitwise_xor(jnp.arange(N_OUTER, dtype=jnp.int32), mask_bits).astype(jnp.int32)


def draw_swap_ids(key, part):
    mask_bits = pair_mask(key)
    n_blocks = TOK_DEV // BLK
    scores = jax.random.randint(jax.random.fold_in(key, 12), (N_OUTER, N_INNER, n_blocks), 0, 1 << 20, dtype=jnp.int32)
    scores = scores * n_blocks + jnp.arange(n_blocks, dtype=jnp.int32)
    order = jnp.argsort(scores, axis=-1, stable=True)[:, :, :NSWAP]
    order = jnp.sort(order, axis=-1).astype(jnp.int32)
    seq_ids = jnp.arange(N_OUTER, dtype=jnp.int32)
    lower = jnp.minimum(seq_ids, jnp.bitwise_xor(seq_ids, mask_bits))
    return order[lower].astype(jnp.int32)


def key_rows(key):
    return jax.random.truncated_normal(jax.random.fold_in(key, 21), -4.0, 4.0, (TOKEN_TOTAL, KEY_VALUE_HEADS, HEAD_SIZE), jnp.float32)


def draw_key_values(key, part):
    key_matrix = key_rows(key)
    base_offset = jax.random.truncated_normal(jax.random.fold_in(key, 23), -4.0, 4.0, (TOKEN_TOTAL, KEY_VALUE_HEADS, HEAD_SIZE), jnp.float32)
    row_scale = jnp.exp(jax.random.uniform(jax.random.fold_in(key, 25), (TOKEN_TOTAL, 1, 1), jnp.float32, jnp.log(0.5), jnp.log(5.0)))
    column_scale = jnp.exp(jax.random.uniform(jax.random.fold_in(key, 26), (1, KEY_VALUE_HEADS, HEAD_SIZE), jnp.float32, jnp.log(0.3), jnp.log(3.0)))
    value_matrix = base_offset * row_scale * column_scale
    return jnp.stack([key_matrix, value_matrix], axis=2).reshape(TOKEN_TOTAL, KEY_VALUE_HEADS * 2 * HEAD_SIZE).astype(jnp.bfloat16)


def draw_queries(key, part):
    portion_each = QUERY_HEADS // KEY_VALUE_HEADS
    base_offset = jax.random.truncated_normal(jax.random.fold_in(key, 31), -4.0, 4.0, (TOKEN_TOTAL, KEY_VALUE_HEADS, portion_each, HEAD_SIZE), jnp.float32)
    return base_offset.reshape(TOKEN_TOTAL, QUERY_HEADS * HEAD_SIZE).astype(jnp.bfloat16)


def length_profile(number_of, total, most, slope):
    loads = [(1 << 20) // math.isqrt(grade ** slope) + 1 for grade in range(2, number_of + 1)]
    spare, given = total - most - (number_of - 1), [1] * (number_of - 1)
    while spare > 0:
        candidates = [i for i in range(number_of - 1) if given[i] < most]
        mass, remaining = sum([loads[i] for i in candidates]), spare
        for i in candidates:
            addition = min(most - given[i], max(1, remaining * loads[i] // mass), spare)
            given[i] = given[i] + addition
            spare = spare - addition
    return np.array([most] + given)


def uneven_parts(key, number_of, total, bound, skew):
    if number_of == 2:
        one = jax.random.randint(key, (), max(1, total - bound), min(bound, total - 1) + 1)
        return jnp.stack([one, total - one])
    sizes = jnp.asarray(length_profile(number_of, total, bound, skew), jnp.int32)
    pairs = (number_of - 1) // 2
    source_of, taker = sizes[1:1 + 2 * pairs:2], sizes[2:2 + 2 * pairs:2]
    slack = jnp.minimum(source_of - 1, bound - taker)
    passed = jax.random.randint(jax.random.fold_in(key, 1), (pairs,), 0, 1 << 20) % (slack + 1)
    sizes = sizes.at[1:1 + 2 * pairs:2].set(source_of - passed).at[2:2 + 2 * pairs:2].set(taker + passed)
    return sizes[jax.random.permutation(jax.random.fold_in(key, 2), number_of)]


def deal_out(key, own, number, rows, number_of, top, most, skew):
    order = jax.random.permutation(key, number_of)
    crowded, usual = shares(number_of, rows * top, most, skew, True), shares(number_of, rows * top, most, skew, False)
    places = jnp.arange(number_of)

    def named(sizes, turn):
        used = int((sizes > 0).sum())
        fixed = max(1, used // 4)
        passed = fixed + (places - fixed + turn * (used - fixed)) % max(1, number_of - fixed)
        return jnp.zeros((number_of,), jnp.int32).at[order[jnp.where(places < fixed, places, passed)]].set(jnp.asarray(sizes, jnp.int32))

    sizes = jnp.where(number % 4 == 0, named(crowded, number // 4), named(usual, number - number // 4 - 1))
    mixed = jax.random.permutation(jax.random.fold_in(own, 3), number_of)
    source_of, taker = mixed[0:number_of // 2 * 2:2], mixed[1:number_of // 2 * 2:2]
    room = jnp.minimum(sizes[source_of] - 1, most - sizes[taker]) // 2
    room = jnp.where((source_of == order[0]) | (taker == order[0]) | (sizes[taker] == 0), 0, jnp.maximum(room, 0))
    passed = jax.random.randint(jax.random.fold_in(own, 4), (number_of // 2,), 0, 1 << 20) % (room + 1)
    sizes = sizes.at[source_of].add(-passed).at[taker].add(passed)
    members = jnp.searchsorted(jnp.cumsum(sizes), jnp.arange(rows * top), side="right").astype(jnp.int32)
    listing = members.reshape(top, rows).T
    listing = listing[jax.random.permutation(jax.random.fold_in(own, 1), rows)]
    turn = jax.random.randint(jax.random.fold_in(own, 2), (rows, 1), 0, top)
    return jnp.take_along_axis(listing, (jnp.arange(top)[None, :] + turn) % top, axis=1)


def shares(count, total, bound, skew, full):
    portions = [(1 << 20) // math.isqrt(rank ** skew) + 1 for rank in range(1, count + 1)]
    largest = bound if full else min(bound, max(-(-total // count), total * portions[0] // sum(portions)))
    least = 1 if total - largest >= count - 1 else 0
    given, spare = [largest] + [least] * (count - 1), total - largest - least * (count - 1)
    while spare > 0:
        movable = [i for i in range(1, count) if given[i] < largest] or [i for i in range(1, count) if given[i] < bound]
        pool, remaining = sum([portions[i] for i in movable]), spare
        for i in movable:
            addition = min(bound - given[i], max(1, remaining * portions[i] // pool), spare)
            given[i] = given[i] + addition
            spare = spare - addition
    return np.array(given)


def setup_inputs(seed: int = 0) -> dict:
    arg_keys = jax.random.split(jax.random.key(seed), 8)
    queries = draw_queries(jax.random.fold_in(arg_keys[7], 71), 0)
    key_values = draw_key_values(jax.random.fold_in(arg_keys[7], 71), 0)
    doc_lengths = jax.vmap(lambda own: uneven_parts(own, NDOCS, GROUP, GROUP // 2, 2))(jax.random.split(arg_keys[2], N_OUTER)).reshape((N_OUTER, NDOCS)).astype(jnp.int32)
    pairing = draw_pairing(jax.random.fold_in(arg_keys[7], 71), 0)
    swap_ids = draw_swap_ids(jax.random.fold_in(arg_keys[7], 71), 0)
    dest_keys = jax.random.split(jax.random.fold_in(arg_keys[5], 1), TOKEN_TOTAL // TOK_DEV)
    dest_turns = jax.random.permutation(jax.random.fold_in(arg_keys[5], 3), TOKEN_TOTAL // TOK_DEV)
    dest = jax.vmap(lambda own, number: deal_out(jax.random.fold_in(arg_keys[5], 2), own, number, TOK_DEV, N_INNER, 1, CAP, 2))(dest_keys, dest_turns).reshape((TOKEN_TOTAL, 1))
    gain = jnp.clip(1.0 + 0.18 * jax.random.normal(arg_keys[6], (QUERY_HEADS * HEAD_SIZE,), jnp.float32), 0.1, 1.9)
    return {"queries": queries, "key_values": key_values, "doc_lengths": doc_lengths, "pairing": pairing, "swap_ids": swap_ids, "dest": dest, "gain": gain}


def doc_index(positions, lengths):
    ends = jnp.cumsum(lengths)
    return lax.optimization_barrier(jnp.sum((positions[:, None] >= ends[None, :]).astype(jnp.int32), axis=1))

def normalize(row_list, gain):
    value_matrix = row_list.astype(jnp.float32)
    factor = lax.rsqrt(lax.optimization_barrier(jnp.mean(value_matrix * value_matrix, axis=-1, keepdims=True)) + 1e-06)
    return (value_matrix * factor * gain).astype(jnp.bfloat16)

def reference(queries, key_values, doc_lengths, pairing, swap_ids, dest, gain):
    width = QUERY_HEADS * HEAD_SIZE
    key_value_width = KEY_VALUE_HEADS * 2 * HEAD_SIZE
    n_blocks = TOK_DEV // BLK
    grouped_row_list = N_INNER * TOK_DEV
    portion_each = QUERY_HEADS // KEY_VALUE_HEADS
    scale = 1.0 / math.sqrt(HEAD_SIZE)
    q_groups = queries.reshape(N_OUTER, N_INNER, n_blocks, BLK, width)
    kv_groups = key_values.reshape(N_OUTER, N_INNER, n_blocks, BLK, key_value_width)
    dest_groups = dest[:, 0].reshape(N_OUTER, N_INNER, TOK_DEV)
    positions = jnp.arange(grouped_row_list, dtype=jnp.int32)
    q_block = min(256, grouped_row_list)
    block_ids = jnp.arange(n_blocks, dtype=jnp.int32)
    inner_ids = jnp.arange(N_INNER, dtype=jnp.int32)

    def one_group(g):
        partner = pairing[g]
        listed = jnp.any(swap_ids[g][:, :, None] == block_ids[None, None, :], axis=1)
        chosen = listed[:, :, None, None]
        query_sequence = jnp.where(chosen, q_groups[partner], q_groups[g]).reshape(grouped_row_list, width)
        key_value_sequence = jnp.where(chosen, kv_groups[partner], kv_groups[g]).reshape(grouped_row_list, key_value_width)
        docs = doc_index(positions, doc_lengths[g])
        query_4 = query_sequence.reshape(grouped_row_list, KEY_VALUE_HEADS, portion_each, HEAD_SIZE).astype(jnp.float32)
        key_value_4 = key_value_sequence.reshape(grouped_row_list, KEY_VALUE_HEADS, 2, HEAD_SIZE).astype(jnp.float32)
        key_matrix = key_value_4[:, :, 0]
        value_matrix = key_value_4[:, :, 1]

        def one_block(index):
            start = index * q_block
            q_blk = lax.dynamic_slice_in_dim(query_4, start, q_block, 0)
            q_pos = start + jnp.arange(q_block, dtype=jnp.int32)
            q_doc = lax.dynamic_slice_in_dim(docs, start, q_block, 0)
            scores = jnp.einsum('qkgd,rkd->kgqr', q_blk, key_matrix) * scale
            allowed = (positions[None, :] <= q_pos[:, None]) & (docs[None, :] == q_doc[:, None])
            scores = jnp.where(allowed, scores, -1e+30)
            top = lax.optimization_barrier(jnp.max(scores, axis=-1, keepdims=True))
            expo = jnp.where(allowed, jnp.exp(scores - top), 0.0)
            total = lax.optimization_barrier(jnp.sum(expo, axis=-1))
            weights = lax.optimization_barrier(expo.astype(jnp.bfloat16)).astype(jnp.float32)
            numer = jnp.einsum('kgqr,rkd->qkgd', weights, value_matrix)
            result = numer / jnp.transpose(total, (2, 0, 1))[..., None]
            return result.astype(jnp.bfloat16).reshape(q_block, width)
        attn = lax.map(one_block, jnp.arange(grouped_row_list // q_block, dtype=jnp.int32)).reshape(grouped_row_list, width)
        normed = normalize(attn, gain)
        dest_g = dest_groups[g]
        onehot = (dest_g[:, :, None] == inner_ids[None, None, :]).astype(jnp.int32)
        rank = lax.optimization_barrier(jnp.sum(jnp.cumsum(onehot, axis=1) * onehot, axis=2)) - 1
        place = ((dest_g * N_INNER + inner_ids[:, None]) * CAP + rank).reshape(grouped_row_list).astype(jnp.int32)
        return jnp.zeros((N_INNER * N_INNER * CAP, width), jnp.bfloat16).at[place].set(normed)
    result = lax.map(one_group, jnp.arange(N_OUTER, dtype=jnp.int32))
    return result.reshape(N_OUTER * N_INNER * N_INNER * CAP, width)
```

```python
import functools
import math

import jax
import jax.numpy as jnp
from jax import lax
from jax.experimental import pallas as pl
from jax.experimental.pallas import tpu as pltpu
from jax.sharding import PartitionSpec as P

QUERY_HEADS = 40
KEY_VALUE_HEADS = 8
PORTION = QUERY_HEADS // KEY_VALUE_HEADS
HEAD_SIZE = 128
BLK = 32
NSWAP = 2

NEGATIVE_LARGE = -1e30
HEAD_GROUPS = (4, 4)
VMEM_LIMIT = 48 * 1024 * 1024


def params():
    return pltpu.CompilerParams(vmem_limit_bytes=VMEM_LIMIT)


def ring(step, size):
    return [(i, (i + step) % size) for i in range(size)]


def from_partner(value, level, size):
    return lax.ppermute(value, "outer", [(i, i ^ (1 << level)) for i in range(size)])


def block_order(listed, n_blocks):
    ids = jnp.arange(n_blocks, dtype=jnp.int32)
    is_listed = jnp.any(ids[:, None] == listed[None, :], axis=1).astype(jnp.int32)
    place = jnp.where(
        is_listed == 1,
        n_blocks - listed.shape[0] + jnp.cumsum(is_listed) - 1,
        jnp.cumsum(1 - is_listed) - 1,
    )
    return jnp.sum(jnp.where(place[None, :] == ids[:, None], ids[None, :], 0), axis=1)


def split_kernel(order, q_ref, kv_ref, kv_rest, kv_listed, q_listed, sems):
    n_rest = kv_rest.shape[0] // BLK
    copies = []
    for b in range(kv_ref.shape[0] // BLK):
        here = pl.ds(pl.multiple_of(order[b] * BLK, BLK), BLK)
        if b < n_rest:
            pairs = [(kv_ref, kv_rest, b)]
        else:
            pairs = [(kv_ref, kv_listed, b - n_rest), (q_ref, q_listed, b - n_rest)]
        for source, target, at in pairs:
            copies.append((source.at[here], target.at[pl.ds(at * BLK, BLK)]))
    copies = [pltpu.make_async_copy(s, t, sems.at[i]) for i, (s, t) in enumerate(copies)]
    for copy in copies:
        copy.start()
    for copy in copies:
        copy.wait()


def split_blocks(order, queries, key_values):
    row_list, width = queries.shape
    kv_width = key_values.shape[1]
    some = NSWAP * BLK
    anywhere = pl.BlockSpec(memory_space=pl.ANY)
    return pl.pallas_call(
        split_kernel,
        out_shape=(
            jax.ShapeDtypeStruct((row_list - some, kv_width), jnp.bfloat16),
            jax.ShapeDtypeStruct((some, kv_width), jnp.bfloat16),
            jax.ShapeDtypeStruct((some, width), jnp.bfloat16),
        ),
        in_specs=[pl.BlockSpec(memory_space=pltpu.SMEM), anywhere, anywhere],
        out_specs=(anywhere,) * 3,
        scratch_shapes=[pltpu.SemaphoreType.DMA((row_list // BLK + NSWAP,))],
        compiler_params=params(),
        name="split_blocks",
    )(order, queries, key_values)


def exchange(listed_rows, pair_bits, n_outer):
    levels = n_outer.bit_length() - 1

    def hop(value, level):
        arrived = from_partner(value, level, n_outer)
        return jnp.where((pair_bits >> level) & 1 == 1, arrived, value)

    value = hop(listed_rows, 0)
    rest = list(range(1, levels))
    turn = (len(rest) + 1) // 2
    halves = []
    for part, order in enumerate((rest, rest[turn:] + rest[:turn])):
        half = value[part * BLK : (part + 1) * BLK]
        for level in order:
            half = hop(half, level)
        halves.append(half)
    return halves


def attend_kernel(n_keys, n_out, order, key_pos, q_pos, q_start, place, q_ref, *refs):
    q_new = refs[:NSWAP]
    kv_refs = refs[NSWAP : NSWAP + n_keys]
    outs = refs[NSWAP + n_keys : NSWAP + n_keys + n_out]
    q_all = refs[-1]
    row_list = q_ref.shape[0]
    capacity = outs[0].shape[0]
    n_rest = row_list // BLK - NSWAP

    q_all[...] = q_ref[...]
    for part in range(NSWAP):
        at = pl.multiple_of(order[n_rest + part] * BLK, BLK)
        q_all[pl.ds(at, BLK), :] = q_new[part][...]

    key = jnp.concatenate([ref[:, :HEAD_SIZE] for ref in kv_refs], axis=0)
    value = jnp.concatenate([ref[:, HEAD_SIZE:] for ref in kv_refs], axis=0)
    query = jnp.concatenate(
        [q_all[:, h * HEAD_SIZE : (h + 1) * HEAD_SIZE] for h in range(PORTION)], axis=0
    )
    scores = lax.dot_general(
        query, key, (((1,), (1,)), ((), ())), preferred_element_type=jnp.float32
    ) * (1.0 / math.sqrt(HEAD_SIZE))
    allowed = (key_pos[...] <= q_pos[...]) & (key_pos[...] >= q_start[...])
    allowed = jnp.concatenate([allowed] * PORTION, axis=0)
    scores = jnp.where(allowed, scores, NEGATIVE_LARGE)
    expo = jnp.exp(scores - jnp.max(scores, axis=1, keepdims=True))
    expo = jnp.where(allowed, expo, 0.0)
    total = jnp.sum(expo, axis=1, keepdims=True)
    attn = jnp.dot(expo.astype(jnp.bfloat16), value, preferred_element_type=jnp.float32)
    attn = (attn / total).astype(jnp.bfloat16)
    attn = jnp.concatenate(
        [attn[h * row_list : (h + 1) * row_list] for h in range(PORTION)], axis=1
    )
    slots = lax.broadcasted_iota(jnp.int32, (n_out * capacity, row_list), 0)
    chosen = (slots == place[...]).astype(jnp.bfloat16)
    routed = jnp.dot(chosen, attn, preferred_element_type=jnp.float32).astype(jnp.bfloat16)
    for k in range(n_out):
        outs[k][...] = routed[k * capacity : (k + 1) * capacity]


def attend(first, heads, order, key_pos, q_pos, q_start, place, queries, q_new, kv_parts, n_out):
    row_list = queries.shape[0]
    capacity = NSWAP * row_list // n_out
    wide = PORTION * HEAD_SIZE
    n_all = sum(part.shape[0] for part in kv_parts)

    def whole(shape):
        return pl.BlockSpec(shape, lambda s: (0, 0))

    def columns(rows, width):
        return pl.BlockSpec((rows, width), lambda s: (0, first + s))

    return pl.pallas_call(
        functools.partial(attend_kernel, len(kv_parts), n_out),
        grid=(heads,),
        out_shape=[jax.ShapeDtypeStruct((capacity, heads * wide), jnp.bfloat16)] * n_out,
        in_specs=[
            pl.BlockSpec(memory_space=pltpu.SMEM),
            whole((1, n_all)),
            whole((row_list, 1)),
            whole((row_list, 1)),
            whole((1, row_list)),
            columns(row_list, wide),
        ]
        + [columns(BLK, wide)] * NSWAP
        + [columns(part.shape[0], 2 * HEAD_SIZE) for part in kv_parts],
        out_specs=[pl.BlockSpec((capacity, wide), lambda s: (0, s))] * n_out,
        scratch_shapes=[pltpu.VMEM((row_list, wide), jnp.bfloat16)],
        compiler_params=params(),
        cost_estimate=pl.CostEstimate(
            flops=heads * PORTION * row_list * n_all * HEAD_SIZE * 4,
            bytes_accessed=heads * (4 * wide * row_list * 2 + n_all * 512),
            transcendentals=heads * PORTION * row_list * n_all,
        ),
        name="attend",
    )(order, key_pos, q_pos, q_start, place, queries, *q_new, *kv_parts)


def norm_kernel(n_inner, n_groups, me, gain, *refs):
    parts = refs[: n_inner * n_groups]
    out = refs[n_inner * n_groups]
    held, ready, in_sems, out_sems = refs[n_inner * n_groups + 1 :]
    capacity, width = parts[0].shape[0], held.shape[2]
    loads = []
    for k in range(n_inner):
        column = 0
        for g in range(n_groups):
            ref = parts[g * n_inner + k]
            wide = ref.shape[1]
            loads.append(
                pltpu.make_async_copy(
                    ref, held.at[k, :, pl.ds(column, wide)], in_sems.at[k, g]
                )
            )
            loads[-1].start()
            column += wide
    stores = []
    for k in range(n_inner):
        for g in range(n_groups):
            loads[k * n_groups + g].wait()
        value = held[k].astype(jnp.float32)
        factor = lax.rsqrt(jnp.sum(value * value, axis=1, keepdims=True) / width + 1e-06)
        ready[k] = (value * factor * gain[...]).astype(jnp.bfloat16)
        source = lax.rem(me[0] - k + n_inner, n_inner)
        there = pl.ds(pl.multiple_of(source * capacity, capacity), capacity)
        stores.append(pltpu.make_async_copy(ready.at[k], out.at[there], out_sems.at[k]))
        stores[-1].start()
    for store in stores:
        store.wait()


def normalize(me, gain, parts, n_inner):
    n_groups = len(parts) // n_inner
    capacity = parts[0].shape[0]
    width = gain.shape[0]
    return pl.pallas_call(
        functools.partial(norm_kernel, n_inner, n_groups),
        out_shape=jax.ShapeDtypeStruct((n_inner * capacity, width), jnp.bfloat16),
        in_specs=[
            pl.BlockSpec(memory_space=pltpu.SMEM),
            pl.BlockSpec((1, width), lambda: (0, 0)),
        ]
        + [pl.BlockSpec(memory_space=pl.ANY)] * len(parts),
        out_specs=pl.BlockSpec(memory_space=pl.ANY),
        scratch_shapes=[
            pltpu.VMEM((n_inner, capacity, width), jnp.bfloat16),
            pltpu.VMEM((n_inner, capacity, width), jnp.bfloat16),
            pltpu.SemaphoreType.DMA((n_inner, n_groups)),
            pltpu.SemaphoreType.DMA((n_inner,)),
        ],
        compiler_params=params(),
        name="normalize",
    )(me.reshape(1), gain.reshape(1, width), *parts)


def shards(queries, key_values, doc_lengths, pairing, swap_ids, dest, gain):
    row_list = queries.shape[0]
    n_inner = lax.axis_size("inner")
    n_outer = lax.axis_size("outer")
    me = lax.axis_index("inner")
    n_blocks = row_list // BLK
    n_back = n_inner // 2
    pair_bits = pairing[0]
    order = block_order(swap_ids[0, 0], n_blocks)

    kv_rest, kv_listed, q_listed = split_blocks(order, queries, key_values)

    rest_parts, orders = [kv_rest], [order]
    for _ in range(n_back):
        rest_parts.append(lax.ppermute(rest_parts[-1], "inner", ring(1, n_inner)))
        orders.append(lax.ppermute(orders[-1], "inner", ring(1, n_inner)))
    kv_new = jnp.concatenate(exchange(kv_listed, pair_bits, n_outer), axis=0)
    listed_parts = [kv_new]
    for _ in range(n_back):
        listed_parts.append(lax.ppermute(listed_parts[-1], "inner", ring(1, n_inner)))
    q_new = exchange(q_listed, pair_bits, n_outer)

    inside = jnp.arange(BLK, dtype=jnp.int32)
    key_pos = []
    for back in range(n_back + 1):
        pos = (orders[back][:, None] * BLK + inside[None, :]).reshape(-1)
        key_pos.append(jnp.where(me >= back, pos + (me - back) * row_list, -1))
    key_pos = jnp.concatenate(key_pos)[None, :]
    q_pos = me * row_list + jnp.arange(row_list, dtype=jnp.int32)
    ends = jnp.cumsum(doc_lengths[0])
    q_start = jnp.max(jnp.where(ends[None, :] <= q_pos[:, None], ends[None, :], 0), axis=1)

    my_dest = dest[:, 0]
    same = my_dest[:, None] == my_dest[None, :]
    earlier = q_pos[None, :] < q_pos[:, None]
    rank = jnp.sum((same & earlier).astype(jnp.int32), axis=1)
    capacity = NSWAP * row_list // n_inner
    place = lax.rem(my_dest - me + n_inner, n_inner) * capacity + rank

    kv_parts = [part for pair in zip(rest_parts, listed_parts) for part in pair]
    arrived, first = [], 0
    for heads in HEAD_GROUPS:
        routed = attend(
            first,
            heads,
            order,
            key_pos,
            q_pos[:, None],
            q_start[:, None],
            place[None, :],
            queries,
            q_new,
            kv_parts,
            n_inner,
        )
        arrived.append(routed[0])
        for k in range(1, n_inner):
            arrived.append(lax.ppermute(routed[k], "inner", ring(k, n_inner)))
        first += heads
    return normalize(me, gain, arrived, n_inner)


def solution(mesh):
    return jax.shard_map(
        shards,
        mesh=mesh,
        in_specs=(
            P(("outer", "inner"), None),
            P(("outer", "inner"), None),
            P("outer", None),
            P(),
            P("outer", "inner", None),
            P(("outer", "inner"), None),
            P(),
        ),
        out_specs=P(("outer", "inner"), None),
        check_vma=False,
    )
```

```python
import functools
import math

import jax
import jax.numpy as jnp
from jax import lax
from jax.experimental import pallas as pl
from jax.experimental.pallas import tpu as pltpu
from jax.sharding import PartitionSpec as P

QUERY_HEADS = 40
KEY_VALUE_HEADS = 8
PORTION = QUERY_HEADS // KEY_VALUE_HEADS
HEAD_SIZE = 128
BLK = 32
NSWAP = 2
LANES = 128

NEGATIVE_LARGE = -1e30
HEAD_GROUPS = (4, 4)
MIB = 1024 * 1024


def params(mib=60):
    return pltpu.CompilerParams(vmem_limit_bytes=mib * MIB)


def ring(step, size):
    return [(i, (i + step) % size) for i in range(size)]


def block_order(listed, n_blocks):
    low, high = listed
    first = jnp.where(low > 0, 0, jnp.where(high > 1, 1, 2))
    return [first, n_blocks * (n_blocks - 1) // 2 - first - low - high, low, high]


def split_kernel(ids, q_ref, kv_ref, kv_rest, kv_listed, q_listed, kv_held, q_held, held_pos, sems):
    n_blocks = kv_ref.shape[0] // BLK
    n_rest = n_blocks - NSWAP
    kv_width = kv_ref.shape[1]
    order = block_order((ids[0, 0, 0], ids[0, 0, 1]), n_blocks)
    moves = []
    for b, block in enumerate(order):
        here = pl.ds(pl.multiple_of(block * BLK, BLK), BLK)
        held = pl.ds(b * BLK, BLK)
        if b < n_rest:
            target = kv_rest.at[held, pl.ds(0, kv_width)]
            moves.append((kv_ref.at[here], kv_held.at[held], target))
        else:
            there = pl.ds((b - n_rest) * BLK, BLK)
            moves.append((kv_ref.at[here], kv_held.at[held], kv_listed.at[there]))
            moves.append((q_ref.at[here], q_held.at[there], q_listed.at[there]))
    loads, stores = [], []
    for i, (source, middle, target) in enumerate(moves):
        loads.append(pltpu.make_async_copy(source, middle, sems.at[0, i]))
        stores.append(pltpu.make_async_copy(middle, target, sems.at[1, i]))
    for load in loads:
        load.start()
    shape = held_pos.shape
    row = lax.broadcasted_iota(jnp.int32, shape, 0)
    lane = lax.broadcasted_iota(jnp.int32, shape, 1)
    pos = jnp.zeros(shape, jnp.int32)
    for b, block in enumerate(order):
        at = b % n_rest * BLK
        here = (row >= at) & (row < at + BLK) & (lane == b // n_rest)
        pos = jnp.where(here, row - at + block * BLK, pos)
    held_pos[...] = pos.astype(jnp.bfloat16)
    tail = kv_rest.at[:, pl.ds(kv_width, LANES)]
    stores.append(pltpu.make_async_copy(held_pos, tail, sems.at[1, len(moves)]))
    stores[-1].start()
    for load, store in zip(loads, stores):
        load.wait()
        store.start()
    for store in stores:
        store.wait()


def split_blocks(swap_ids, queries, key_values):
    row_list, width = queries.shape
    kv_width = key_values.shape[1]
    some = NSWAP * BLK
    far = pl.BlockSpec(memory_space=pl.ANY)
    return pl.pallas_call(
        split_kernel,
        out_shape=(
            jax.ShapeDtypeStruct((row_list - some, kv_width + LANES), jnp.bfloat16),
            jax.ShapeDtypeStruct((some, kv_width), jnp.bfloat16),
            jax.ShapeDtypeStruct((some, width), jnp.bfloat16),
        ),
        in_specs=[pl.BlockSpec(memory_space=pltpu.SMEM), far, far],
        out_specs=(far,) * 3,
        scratch_shapes=[
            pltpu.VMEM((row_list, kv_width), jnp.bfloat16),
            pltpu.VMEM((some, width), jnp.bfloat16),
            pltpu.VMEM((row_list - some, LANES), jnp.bfloat16),
            pltpu.SemaphoreType.DMA((2, row_list // BLK + NSWAP + 1)),
        ],
        compiler_params=params(60),
        name="split_blocks",
    )(swap_ids, queries, key_values)


def back(value, n_inner):
    return lax.ppermute(value, "inner", ring(1, n_inner))


def gather_keys(mask, n_outer, n_inner, n_back, kv_rest, kv_listed, q_listed):
    def swap(value):
        return lax.ppermute(value, "outer", [(i, i ^ mask) for i in range(n_outer)])

    def reach_back(value):
        parts = [value]
        for _ in range(n_back):
            parts.append(back(parts[-1], n_inner))
        return parts

    rest = reach_back(kv_rest)
    listed = reach_back(swap(kv_listed))
    return swap(q_listed), rest[1:], listed


def fill_tables(n_out, lengths, dest, pos_refs, bias, chosen):
    row_list, n_all = bias.shape
    me = lax.axis_index("inner")
    lane = lax.broadcasted_iota(jnp.int32, (1, LANES), 1)
    key_pos = []
    for back, ref in enumerate(pos_refs):
        for which in range(2):
            pick = (lane == which).astype(jnp.bfloat16)
            pos = lax.dot_general(
                pick, ref[...], (((1,), (1,)), ((), ())), preferred_element_type=jnp.float32
            ).astype(jnp.int32)
            key_pos.append(jnp.where(me >= back, pos + (me - back) * row_list, -1))
    key_pos = jnp.concatenate(key_pos, axis=1)
    q_pos = me * row_list + lax.broadcasted_iota(jnp.int32, (row_list, 1), 0)
    end, start = 0, jnp.zeros((row_list, 1), jnp.int32)
    for k in range(lengths.shape[1]):
        end = end + lengths[0, k]
        start = jnp.where(q_pos >= end, end, start)
    bias[...] = jnp.where((key_pos <= q_pos) & (key_pos >= start), 0.0, NEGATIVE_LARGE)

    capacity = chosen.shape[0] // n_out
    square = (row_list, row_list)
    named = lax.broadcasted_iota(jnp.int32, square, 0) == dest[...]
    earlier = lax.broadcasted_iota(jnp.int32, square, 0) < lax.broadcasted_iota(jnp.int32, square, 1)
    before = jnp.dot(
        named.astype(jnp.bfloat16), earlier.astype(jnp.bfloat16), preferred_element_type=jnp.float32
    )
    rank = jnp.sum(jnp.where(named, before, 0.0), axis=0, keepdims=True).astype(jnp.int32)
    place = lax.rem(dest[...] - me + n_out, n_out) * capacity + rank
    slots = lax.broadcasted_iota(jnp.int32, chosen.shape, 0)
    chosen[...] = (slots == place).astype(jnp.bfloat16)


def attend_kernel(n_keys, n_out, ids, lengths, dest, q_ref, q_new, *refs):
    pos_refs = refs[: n_keys // 2]
    kv_refs = refs[n_keys // 2 : n_keys // 2 + n_keys]
    outs = refs[-3 - n_out : -3]
    q_all, bias, chosen = refs[-3:]
    row_list = q_ref.shape[0]
    capacity = outs[0].shape[0]

    @pl.when(pl.program_id(0) == 0)
    def _():
        fill_tables(n_out, lengths, dest, pos_refs, bias, chosen)

    q_all[...] = q_ref[...]
    for part in range(NSWAP):
        at = pl.multiple_of(ids[0, 0, part] * BLK, BLK)
        q_all[pl.ds(at, BLK), :] = q_new[part * BLK : (part + 1) * BLK, :]

    key = jnp.concatenate([ref[:, :HEAD_SIZE] for ref in kv_refs], axis=0)
    value = jnp.concatenate([ref[:, HEAD_SIZE:] for ref in kv_refs], axis=0)
    query = jnp.concatenate(
        [q_all[:, h * HEAD_SIZE : (h + 1) * HEAD_SIZE] for h in range(PORTION)], axis=0
    )
    scores = lax.dot_general(
        query, key, (((1,), (1,)), ((), ())), preferred_element_type=jnp.float32
    )
    scores = scores + jnp.concatenate([bias[...]] * PORTION, axis=0)
    top = jnp.max(scores, axis=1, keepdims=True)
    expo = jnp.exp2((scores - top) * (math.log2(math.e) / math.sqrt(HEAD_SIZE)))
    total = jnp.sum(expo, axis=1, keepdims=True)
    attn = jnp.dot(expo.astype(jnp.bfloat16), value, preferred_element_type=jnp.float32)
    attn = (attn / total).astype(jnp.bfloat16)
    attn = jnp.concatenate(
        [attn[h * row_list : (h + 1) * row_list] for h in range(PORTION)], axis=1
    )
    routed = jnp.dot(chosen[...], attn, preferred_element_type=jnp.float32).astype(jnp.bfloat16)
    for k in range(n_out):
        outs[k][...] = routed[k * capacity : (k + 1) * capacity]


def attend(first, heads, swap_ids, doc_lengths, dest, queries, q_new, kv_parts, n_out, before):
    row_list = queries.shape[0]
    capacity = NSWAP * row_list // n_out
    wide = PORTION * HEAD_SIZE
    tail = KEY_VALUE_HEADS * 2 * HEAD_SIZE // LANES
    n_all = sum(part.shape[0] for part in kv_parts)

    def columns(rows, width):
        return pl.BlockSpec((rows, width), lambda s: (0, first + s))

    return pl.pallas_call(
        functools.partial(attend_kernel, len(kv_parts), n_out),
        grid=(heads,),
        out_shape=[jax.ShapeDtypeStruct((capacity, heads * wide), jnp.bfloat16)] * n_out,
        in_specs=[
            pl.BlockSpec(memory_space=pltpu.SMEM),
            pl.BlockSpec(memory_space=pltpu.SMEM),
            pl.BlockSpec((1, row_list), lambda s: (0, 0)),
            columns(row_list, wide),
            columns(NSWAP * BLK, wide),
        ]
        + [pl.BlockSpec((kv_parts[0].shape[0], LANES), lambda s: (0, tail))] * (len(kv_parts) // 2)
        + [columns(part.shape[0], 2 * HEAD_SIZE) for part in kv_parts]
        + [pl.BlockSpec(memory_space=pl.ANY)] * len(before),
        out_specs=[pl.BlockSpec((capacity, wide), lambda s: (0, s))] * n_out,
        scratch_shapes=[
            pltpu.VMEM((row_list, wide), jnp.bfloat16),
            pltpu.VMEM((row_list, n_all), jnp.float32),
            pltpu.VMEM((n_out * capacity, row_list), jnp.bfloat16),
        ],
        compiler_params=params(16 if before else 60),
        cost_estimate=pl.CostEstimate(
            flops=heads * PORTION * row_list * n_all * HEAD_SIZE * 4,
            bytes_accessed=heads * (4 * wide * row_list * 2 + n_all * 512),
            transcendentals=heads * PORTION * row_list * n_all,
        ),
        name="attend",
    )(swap_ids, doc_lengths, dest, queries, q_new, *kv_parts[::2], *kv_parts, *before)


def norm_kernel(n_inner, n_groups, me, gain, *refs):
    parts = refs[: n_inner * n_groups]
    out = refs[n_inner * n_groups]
    held, ready, in_sems, out_sems = refs[n_inner * n_groups + 1 :]
    capacity, width = parts[0].shape[0], held.shape[2]
    loads = []
    for k in range(n_inner):
        column = 0
        for g in range(n_groups):
            ref = parts[g * n_inner + k]
            wide = ref.shape[1]
            loads.append(
                pltpu.make_async_copy(
                    ref, held.at[k, :, pl.ds(column, wide)], in_sems.at[k, g]
                )
            )
            loads[-1].start()
            column += wide
    stores = []
    for k in range(n_inner):
        for g in range(n_groups):
            loads[k * n_groups + g].wait()
        value = held[k].astype(jnp.float32)
        factor = lax.rsqrt(jnp.sum(value * value, axis=1, keepdims=True) / width + 1e-06)
        ready[k] = (value * factor * gain[...]).astype(jnp.bfloat16)
        source = lax.rem(me[0] - k + n_inner, n_inner)
        there = pl.ds(pl.multiple_of(source * capacity, capacity), capacity)
        stores.append(pltpu.make_async_copy(ready.at[k], out.at[there], out_sems.at[k]))
        stores[-1].start()
    for store in stores:
        store.wait()


def normalize(me, gain, parts, n_inner):
    n_groups = len(parts) // n_inner
    capacity = parts[0].shape[0]
    width = gain.shape[0]
    return pl.pallas_call(
        functools.partial(norm_kernel, n_inner, n_groups),
        out_shape=jax.ShapeDtypeStruct((n_inner * capacity, width), jnp.bfloat16),
        in_specs=[
            pl.BlockSpec(memory_space=pltpu.SMEM),
            pl.BlockSpec((1, width), lambda: (0, 0)),
        ]
        + [pl.BlockSpec(memory_space=pl.ANY)] * len(parts),
        out_specs=pl.BlockSpec(memory_space=pl.ANY),
        scratch_shapes=[
            pltpu.VMEM((n_inner, capacity, width), jnp.bfloat16),
            pltpu.VMEM((n_inner, capacity, width), jnp.bfloat16),
            pltpu.SemaphoreType.DMA((n_inner, n_groups)),
            pltpu.SemaphoreType.DMA((n_inner,)),
        ],
        compiler_params=params(16),
        name="normalize",
    )(me.reshape(1), gain.reshape(1, width), *parts)


def shards(queries, key_values, doc_lengths, pairing, swap_ids, dest, gain):
    n_inner = lax.axis_size("inner")
    n_outer = lax.axis_size("outer")
    me = lax.axis_index("inner")
    n_back = n_inner // 2

    kv_rest, kv_listed, q_listed = split_blocks(swap_ids, queries, key_values)
    branches = [
        functools.partial(gather_keys, mask, n_outer, n_inner, n_back)
        for mask in range(1, n_outer)
    ]
    q_new, rest, listed = lax.switch(pairing[0] - 1, branches, kv_rest, kv_listed, q_listed)
    kv_parts = [part for pair in zip([kv_rest] + rest, listed) for part in pair]

    dest_row = dest.reshape(1, -1)
    arrived, first, before = [], 0, []
    for heads in HEAD_GROUPS:
        routed = attend(
            first, heads, swap_ids, doc_lengths, dest_row, queries, q_new, kv_parts, n_inner, before
        )
        before = [routed[0]]
        arrived.append(routed[0])
        for k in range(1, n_inner):
            arrived.append(lax.ppermute(routed[k], "inner", ring(k, n_inner)))
        first += heads
    return normalize(me, gain, arrived, n_inner)


def solution(mesh):
    return jax.shard_map(
        shards,
        mesh=mesh,
        in_specs=(
            P(("outer", "inner"), None),
            P(("outer", "inner"), None),
            P("outer", None),
            P(),
            P("outer", "inner", None),
            P(("outer", "inner"), None),
            P(),
        ),
        out_specs=P(("outer", "inner"), None),
        check_vma=False,
    )
```

```python
import functools
import math

import jax
import jax.numpy as jnp
from jax import lax
from jax.experimental import pallas as pl
from jax.experimental.pallas import tpu as pltpu
from jax.sharding import PartitionSpec as P

QUERY_HEADS = 40
KEY_VALUE_HEADS = 8
PORTION = QUERY_HEADS // KEY_VALUE_HEADS
HEAD_SIZE = 128
BLK = 32
NSWAP = 2
LANES = 128

NEGATIVE_LARGE = -1e30
HEAD_GROUPS = (2, 6)
PLACE_EARLY = 30_000_000_000
PER_STEP = 2
MIB = 1024 * 1024


def params(mib=60):
    return pltpu.CompilerParams(vmem_limit_bytes=mib * MIB)


def ring(step, size):
    return [(i, (i + step) % size) for i in range(size)]


def block_order(listed, n_blocks):
    low, high = listed
    first = jnp.where(low > 0, 0, jnp.where(high > 1, 1, 2))
    return [first, n_blocks * (n_blocks - 1) // 2 - first - low - high, low, high]


def split_kernel(ids, q_ref, kv_ref, kv_rest, kv_listed, q_listed, sems):
    n_blocks = kv_ref.shape[0] // BLK
    n_rest = n_blocks - NSWAP
    kv_width = kv_ref.shape[1]
    order = block_order((ids[0, 0, 0], ids[0, 0, 1]), n_blocks)
    copies = []
    for b, block in enumerate(order):
        here = pl.ds(pl.multiple_of(block * BLK, BLK), BLK)
        there = pl.ds(b % n_rest * BLK, BLK)
        if b < n_rest:
            pairs = [(kv_ref, kv_rest.at[there, pl.ds(0, kv_width)])]
        else:
            pairs = [(kv_ref, kv_listed.at[there]), (q_ref, q_listed.at[there])]
        for source, target in pairs:
            copies.append(pltpu.make_async_copy(source.at[here], target, sems.at[len(copies)]))
            copies[-1].start()
    shape = (kv_rest.shape[0], LANES)
    row = lax.broadcasted_iota(jnp.int32, shape, 0)
    lane = lax.broadcasted_iota(jnp.int32, shape, 1)
    pos = jnp.zeros(shape, jnp.int32)
    for b, block in enumerate(order):
        at = b % n_rest * BLK
        here = (row >= at) & (row < at + BLK) & (lane == b // n_rest)
        pos = jnp.where(here, row - at + block * BLK, pos)
    kv_rest[:, kv_width:] = pos.astype(jnp.bfloat16)
    for copy in copies:
        copy.wait()


def split_blocks(swap_ids, queries, key_values):
    row_list, width = queries.shape
    kv_width = key_values.shape[1]
    some = NSWAP * BLK
    far = pl.BlockSpec(memory_space=pltpu.HBM)
    near = pl.BlockSpec(memory_space=pltpu.VMEM)
    return pl.pallas_call(
        split_kernel,
        out_shape=(
            pltpu.VMEM((row_list - some, kv_width + LANES), jnp.bfloat16),
            pltpu.VMEM((some, kv_width), jnp.bfloat16),
            pltpu.VMEM((some, width), jnp.bfloat16),
        ),
        in_specs=[pl.BlockSpec(memory_space=pltpu.SMEM), far, far],
        out_specs=(near,) * 3,
        scratch_shapes=[pltpu.SemaphoreType.DMA((row_list // BLK + NSWAP,))],
        compiler_params=params(16),
        name="split_blocks",
    )(
        pltpu.with_memory_space_constraint(swap_ids, pltpu.HBM),
        pltpu.with_memory_space_constraint(queries, pltpu.HBM),
        pltpu.with_memory_space_constraint(key_values, pltpu.HBM),
    )


def back(value, n_inner):
    return lax.ppermute(value, "inner", ring(1, n_inner))


def gather_keys(mask, n_outer, n_inner, n_back, doc_lengths, dest, kv_rest, kv_listed, q_listed):
    def swap(value):
        return lax.ppermute(value, "outer", [(i, i ^ mask) for i in range(n_outer)])

    def reach_back(value):
        parts = [value]
        for _ in range(n_back):
            parts.append(back(parts[-1], n_inner))
        return parts

    rest = reach_back(kv_rest)
    listed = reach_back(swap(kv_listed))
    row_list = dest.shape[1]
    n_all = (n_back + 1) * row_list
    bias, chosen = tables(doc_lengths, dest, rest, row_list, n_all, n_inner)
    return swap(q_listed), rest[1:], listed, bias, chosen


def fill_tables(n_out, lengths, dest, pos_refs, bias, chosen):
    row_list, n_all = bias.shape
    me = lax.axis_index("inner")
    lane = lax.broadcasted_iota(jnp.int32, (1, LANES), 1)
    key_pos = []
    for back, ref in enumerate(pos_refs):
        for which in range(2):
            pick = (lane == which).astype(jnp.bfloat16)
            pos = lax.dot_general(
                pick, ref[...], (((1,), (1,)), ((), ())), preferred_element_type=jnp.float32
            ).astype(jnp.int32)
            key_pos.append(jnp.where(me >= back, pos + (me - back) * row_list, -1))
    key_pos = jnp.concatenate(key_pos, axis=1)
    q_pos = me * row_list + lax.broadcasted_iota(jnp.int32, (row_list, 1), 0)
    end, start = 0, jnp.zeros((row_list, 1), jnp.int32)
    for k in range(lengths.shape[1]):
        end = end + lengths[0, k]
        start = jnp.where(q_pos >= end, end, start)
    bias[...] = jnp.where((key_pos <= q_pos) & (key_pos >= start), 0.0, NEGATIVE_LARGE)

    capacity = chosen.shape[0] // n_out
    square = (row_list, row_list)
    named = lax.broadcasted_iota(jnp.int32, square, 0) == dest[...]
    earlier = lax.broadcasted_iota(jnp.int32, square, 0) < lax.broadcasted_iota(jnp.int32, square, 1)
    before = jnp.dot(
        named.astype(jnp.bfloat16), earlier.astype(jnp.bfloat16), preferred_element_type=jnp.float32
    )
    rank = jnp.sum(jnp.where(named, before, 0.0), axis=0, keepdims=True).astype(jnp.int32)
    place = lax.rem(dest[...] - me + n_out, n_out) * capacity + rank
    slots = lax.broadcasted_iota(jnp.int32, chosen.shape, 0)
    chosen[...] = (slots == place).astype(jnp.bfloat16)


def tables_kernel(n_ranges, n_out, lengths, dest, *refs):
    fill_tables(n_out, lengths, dest, refs[:n_ranges], *refs[n_ranges:])


def tables(doc_lengths, dest, rest, row_list, n_all, n_out):
    capacity = NSWAP * row_list // n_out
    tail = rest[0].shape[1] // LANES - 1
    shapes = ((row_list, n_all), (n_out * capacity, row_list))
    return pl.pallas_call(
        functools.partial(tables_kernel, len(rest), n_out),
        grid=(1,),
        out_shape=(
            jax.ShapeDtypeStruct(shapes[0], jnp.float32),
            jax.ShapeDtypeStruct(shapes[1], jnp.bfloat16),
        ),
        in_specs=[
            pl.BlockSpec(memory_space=pltpu.SMEM),
            pl.BlockSpec((1, row_list), lambda s: (0, 0)),
        ]
        + [pl.BlockSpec((part.shape[0], LANES), lambda s: (0, tail)) for part in rest],
        out_specs=[pl.BlockSpec(shape, lambda s: (0, 0)) for shape in shapes],
        compiler_params=params(16),
        name="tables",
    )(doc_lengths, dest, *rest)


def attend_kernel(n_keys, n_out, ids, q_ref, q_new, bias, chosen, *refs):
    kv_refs = refs[:n_keys]
    outs = refs[-1 - n_out : -1]
    q_all = refs[-1]
    row_list = q_ref.shape[0]
    capacity = outs[0].shape[0]

    q_all[...] = q_ref[...]
    for part in range(NSWAP):
        at = pl.multiple_of(ids[0, 0, part] * BLK, BLK)
        q_all[pl.ds(at, BLK), :] = q_new[part * BLK : (part + 1) * BLK, :]

    for j in range(PER_STEP):
        wide = PORTION * HEAD_SIZE
        at = slice(j * 2 * HEAD_SIZE, (j + 1) * 2 * HEAD_SIZE)
        key = jnp.concatenate([ref[:, at.start : at.start + HEAD_SIZE] for ref in kv_refs], axis=0)
        value = jnp.concatenate([ref[:, at.start + HEAD_SIZE : at.stop] for ref in kv_refs], axis=0)
        first = j * PORTION
        query = jnp.concatenate(
            [
                q_all[:, (first + h) * HEAD_SIZE : (first + h + 1) * HEAD_SIZE]
                for h in range(PORTION)
            ],
            axis=0,
        )
        scores = lax.dot_general(
            query, key, (((1,), (1,)), ((), ())), preferred_element_type=jnp.float32
        )
        scores = scores + jnp.concatenate([bias[...]] * PORTION, axis=0)
        top = jnp.max(scores, axis=1, keepdims=True)
        expo = jnp.exp2((scores - top) * (math.log2(math.e) / math.sqrt(HEAD_SIZE)))
        total = jnp.sum(expo, axis=1, keepdims=True)
        attn = jnp.dot(expo.astype(jnp.bfloat16), value, preferred_element_type=jnp.float32)
        attn = (attn / total).astype(jnp.bfloat16)
        attn = jnp.concatenate(
            [attn[h * row_list : (h + 1) * row_list] for h in range(PORTION)], axis=1
        )
        routed = jnp.dot(chosen[...], attn, preferred_element_type=jnp.float32).astype(jnp.bfloat16)
        for k in range(n_out):
            outs[k][:, j * wide : (j + 1) * wide] = routed[k * capacity : (k + 1) * capacity]


def attend(first, heads, swap_ids, queries, q_new, bias, chosen, kv_parts, before):
    row_list, n_all = bias.shape
    n_out = lax.axis_size("inner")
    capacity = NSWAP * row_list // n_out
    wide = PORTION * HEAD_SIZE

    def columns(rows, width):
        return pl.BlockSpec((rows, width), lambda s: (0, first // PER_STEP + s))

    def whole(array):
        return pl.BlockSpec(array.shape, lambda s: (0, 0))

    return pl.pallas_call(
        functools.partial(attend_kernel, len(kv_parts), n_out),
        grid=(heads // PER_STEP,),
        out_shape=[jax.ShapeDtypeStruct((capacity, heads * wide), jnp.bfloat16)] * n_out,
        in_specs=[
            pl.BlockSpec(memory_space=pltpu.SMEM),
            columns(row_list, PER_STEP * wide),
            columns(NSWAP * BLK, PER_STEP * wide),
            whole(bias),
            whole(chosen),
        ]
        + [columns(part.shape[0], PER_STEP * 2 * HEAD_SIZE) for part in kv_parts]
        + [pl.BlockSpec(memory_space=pl.ANY)] * len(before),
        out_specs=[pl.BlockSpec((capacity, PER_STEP * wide), lambda s: (0, s))] * n_out,
        scratch_shapes=[pltpu.VMEM((row_list, PER_STEP * wide), jnp.bfloat16)],
        compiler_params=params(16 if before else 60),
        cost_estimate=pl.CostEstimate(
            flops=heads * PORTION * row_list * n_all * HEAD_SIZE * 4,
            bytes_accessed=heads * (4 * wide * row_list * 2 + n_all * 512),
            transcendentals=heads * PORTION * row_list * n_all,
        ),
        name="attend",
    )(swap_ids, queries, q_new, bias, chosen, *kv_parts, *before)


def squares_kernel(*refs):
    n_parts = len(refs) // 2
    for ref, out in zip(refs[:n_parts], refs[n_parts:]):
        value = ref[...].astype(jnp.float32)
        out[...] = jnp.broadcast_to(jnp.sum(value * value, axis=1, keepdims=True), out.shape)


def squares(parts):
    capacity, wide = parts[0].shape
    return pl.pallas_call(
        squares_kernel,
        out_shape=[jax.ShapeDtypeStruct((capacity, LANES), jnp.float32)] * len(parts),
        compiler_params=params(16),
        cost_estimate=pl.CostEstimate(
            flops=PLACE_EARLY,
            bytes_accessed=len(parts) * capacity * wide * 2,
            transcendentals=0,
        ),
        name="squares",
    )(*parts)


def norm_kernel(me, gain, early, first, others, *refs):
    out = refs[-1]
    first, others = first[...].astype(jnp.float32), others[...].astype(jnp.float32)
    cut, width = first.shape[1], out.shape[1]
    total = early[...][:, :1] + jnp.sum(others * others, axis=1, keepdims=True)
    factor = lax.rsqrt(total / width + 1e-06)
    out[:, :cut] = (first * factor * gain[:, :cut]).astype(jnp.bfloat16)
    out[:, cut:] = (others * factor * gain[:, cut:]).astype(jnp.bfloat16)


def normalize(source, gain, early, first, others, n_inner, result):
    capacity, cut = first.shape
    width = gain.shape[0]
    steps = 2
    rows = capacity // steps
    held = [] if result is None else [result]
    return pl.pallas_call(
        norm_kernel,
        out_shape=jax.ShapeDtypeStruct((n_inner * capacity, width), jnp.bfloat16),
        grid_spec=pltpu.PrefetchScalarGridSpec(
            num_scalar_prefetch=1,
            grid=(steps,),
            in_specs=[
                pl.BlockSpec((1, width), lambda s, at: (0, 0)),
                pl.BlockSpec((rows, LANES), lambda s, at: (s, 0)),
                pl.BlockSpec((rows, cut), lambda s, at: (s, 0)),
                pl.BlockSpec((rows, width - cut), lambda s, at: (s, 0)),
            ]
            + [pl.BlockSpec(memory_space=pl.ANY)] * len(held),
            out_specs=pl.BlockSpec((rows, width), lambda s, at: (at[0] * steps + s, 0)),
        ),
        input_output_aliases={5: 0} if held else {},
        compiler_params=params(16),
        name="normalize",
    )(source.reshape(1), gain.reshape(1, width), early, first, others, *held)


def shards(queries, key_values, doc_lengths, pairing, swap_ids, dest, gain):
    n_inner = lax.axis_size("inner")
    n_outer = lax.axis_size("outer")
    me = lax.axis_index("inner")
    n_back = n_inner // 2

    kv_rest, kv_listed, q_listed = split_blocks(swap_ids, queries, key_values)
    branches = [
        functools.partial(gather_keys, mask, n_outer, n_inner, n_back)
        for mask in range(1, n_outer)
    ]
    q_new, rest, listed, bias, chosen = lax.switch(
        pairing[0] - 1, branches, doc_lengths, dest.reshape(1, -1), kv_rest, kv_listed, q_listed
    )
    kv_parts = [part for pair in zip([kv_rest] + rest, listed) for part in pair]

    arrived, first, before = [], 0, []
    for heads in HEAD_GROUPS:
        routed = attend(
            first, heads, swap_ids, queries, q_new, bias, chosen, kv_parts, before
        )
        before = [routed[0]]
        arrived.append(routed[0])
        for k in range(1, n_inner):
            arrived.append(lax.ppermute(routed[k], "inner", ring(k, n_inner)))
        first += heads
    early = squares(arrived[:n_inner])
    result = None
    for k in range(n_inner):
        source = lax.rem(me - k + n_inner, n_inner)
        result = normalize(
            source, gain, early[k], arrived[k], arrived[n_inner + k], n_inner, result
        )
    return result


def solution(mesh):
    return jax.shard_map(
        shards,
        mesh=mesh,
        in_specs=(
            P(("outer", "inner"), None),
            P(("outer", "inner"), None),
            P("outer", None),
            P(),
            P("outer", "inner", None),
            P(("outer", "inner"), None),
            P(),
        ),
        out_specs=P(("outer", "inner"), None),
        check_vma=False,
    )
```

```python
import functools
import math

import jax
import jax.numpy as jnp
from jax import lax
from jax.experimental import pallas as pl
from jax.experimental.pallas import tpu as pltpu
from jax.sharding import PartitionSpec as P

QUERY_HEADS = 40
KEY_VALUE_HEADS = 8
PORTION = QUERY_HEADS // KEY_VALUE_HEADS
HEAD_SIZE = 128
BLK = 32
NSWAP = 2
LANES = 128

NEGATIVE_LARGE = -1e30
HEAD_GROUPS = (2, 6)
PLACE_EARLY = 30_000_000_000
PER_STEP = 2
MIB = 1024 * 1024


def params(mib=60):
    return pltpu.CompilerParams(vmem_limit_bytes=mib * MIB)


def ring(step, size):
    return [(i, (i + step) % size) for i in range(size)]


def block_order(listed, n_blocks):
    low, high = listed
    first = jnp.where(low > 0, 0, jnp.where(high > 1, 1, 2))
    return [first, n_blocks * (n_blocks - 1) // 2 - first - low - high, low, high]


def split_kernel(ids, q_ref, kv_ref, kv_rest, kv_listed, q_listed, sems):
    n_blocks = kv_ref.shape[0] // BLK
    n_rest = n_blocks - NSWAP
    kv_width = kv_ref.shape[1]
    order = block_order((ids[0, 0, 0], ids[0, 0, 1]), n_blocks)
    copies = []
    for b, block in enumerate(order):
        here = pl.ds(pl.multiple_of(block * BLK, BLK), BLK)
        there = pl.ds(b % n_rest * BLK, BLK)
        if b < n_rest:
            pairs = [(kv_ref, kv_rest.at[there, pl.ds(0, kv_width)])]
        else:
            pairs = [(kv_ref, kv_listed.at[there]), (q_ref, q_listed.at[there])]
        for source, target in pairs:
            copies.append(pltpu.make_async_copy(source.at[here], target, sems.at[len(copies)]))
            copies[-1].start()
    shape = (kv_rest.shape[0], LANES)
    row = lax.broadcasted_iota(jnp.int32, shape, 0)
    lane = lax.broadcasted_iota(jnp.int32, shape, 1)
    pos = jnp.zeros(shape, jnp.int32)
    for b, block in enumerate(order):
        at = b % n_rest * BLK
        here = (row >= at) & (row < at + BLK) & (lane == b // n_rest)
        pos = jnp.where(here, row - at + block * BLK, pos)
    kv_rest[:, kv_width:] = pos.astype(jnp.bfloat16)
    for copy in copies:
        copy.wait()


def split_blocks(swap_ids, queries, key_values):
    row_list, width = queries.shape
    kv_width = key_values.shape[1]
    some = NSWAP * BLK
    far = pl.BlockSpec(memory_space=pltpu.HBM)
    near = pl.BlockSpec(memory_space=pltpu.VMEM)
    return pl.pallas_call(
        split_kernel,
        out_shape=(
            pltpu.VMEM((row_list - some, kv_width + LANES), jnp.bfloat16),
            pltpu.VMEM((some, kv_width), jnp.bfloat16),
            pltpu.VMEM((some, width), jnp.bfloat16),
        ),
        in_specs=[pl.BlockSpec(memory_space=pltpu.SMEM), far, far],
        out_specs=(near,) * 3,
        scratch_shapes=[pltpu.SemaphoreType.DMA((row_list // BLK + NSWAP,))],
        compiler_params=params(16),
        name="split_blocks",
    )(
        pltpu.with_memory_space_constraint(swap_ids, pltpu.HBM),
        pltpu.with_memory_space_constraint(queries, pltpu.HBM),
        pltpu.with_memory_space_constraint(key_values, pltpu.HBM),
    )


def back(value, n_inner, step):
    pairs = ring(1, n_inner) if step == 1 else [(i, i + 1) for i in range(step - 1, n_inner - 1)]
    return lax.ppermute(value, "inner", pairs)


def gather_keys(mask, n_outer, n_inner, n_back, doc_lengths, dest, kv_rest, kv_listed, q_listed):
    def cross(value, bits):
        return lax.ppermute(value, "outer", [(i, i ^ bits) for i in range(n_outer)])

    def swap(value):
        if mask & 1 and mask > 1:
            return cross(cross(value, 1), mask - 1)
        return cross(value, mask)

    def reach_back(value):
        parts = [value]
        for _ in range(n_back):
            parts.append(back(parts[-1], n_inner, len(parts)))
        return parts

    rest = reach_back(kv_rest)
    listed = reach_back(swap(kv_listed))
    row_list = dest.shape[1]
    n_all = (n_back + 1) * row_list
    bias, chosen = tables(doc_lengths, dest, rest, row_list, n_all, n_inner)
    return swap(q_listed), rest[1:], listed, bias, chosen


def fill_tables(n_out, lengths, dest, pos_refs, bias, chosen):
    row_list, n_all = bias.shape
    me = lax.axis_index("inner")
    lane = lax.broadcasted_iota(jnp.int32, (1, LANES), 1)
    key_pos = []
    for back, ref in enumerate(pos_refs):
        for which in range(2):
            pick = (lane == which).astype(jnp.bfloat16)
            pos = lax.dot_general(
                pick, ref[...], (((1,), (1,)), ((), ())), preferred_element_type=jnp.float32
            ).astype(jnp.int32)
            key_pos.append(jnp.where(me >= back, pos + (me - back) * row_list, -1))
    key_pos = jnp.concatenate(key_pos, axis=1)
    q_pos = me * row_list + lax.broadcasted_iota(jnp.int32, (row_list, 1), 0)
    end, start = 0, jnp.zeros((row_list, 1), jnp.int32)
    for k in range(lengths.shape[1]):
        end = end + lengths[0, k]
        start = jnp.where(q_pos >= end, end, start)
    bias[...] = jnp.where((key_pos <= q_pos) & (key_pos >= start), 0.0, NEGATIVE_LARGE)

    capacity = chosen.shape[0] // n_out
    square = (row_list, row_list)
    named = lax.broadcasted_iota(jnp.int32, square, 0) == dest[...]
    earlier = lax.broadcasted_iota(jnp.int32, square, 0) < lax.broadcasted_iota(jnp.int32, square, 1)
    before = jnp.dot(
        named.astype(jnp.bfloat16), earlier.astype(jnp.bfloat16), preferred_element_type=jnp.float32
    )
    rank = jnp.sum(jnp.where(named, before, 0.0), axis=0, keepdims=True).astype(jnp.int32)
    place = lax.rem(dest[...] - me + n_out, n_out) * capacity + rank
    slots = lax.broadcasted_iota(jnp.int32, chosen.shape, 0)
    chosen[...] = (slots == place).astype(jnp.bfloat16)


def tables_kernel(n_ranges, n_out, lengths, dest, *refs):
    fill_tables(n_out, lengths, dest, refs[:n_ranges], *refs[n_ranges:])


def tables(doc_lengths, dest, rest, row_list, n_all, n_out):
    capacity = NSWAP * row_list // n_out
    tail = rest[0].shape[1] // LANES - 1
    shapes = ((row_list, n_all), (n_out * capacity, row_list))
    return pl.pallas_call(
        functools.partial(tables_kernel, len(rest), n_out),
        grid=(1,),
        out_shape=(
            jax.ShapeDtypeStruct(shapes[0], jnp.float32),
            jax.ShapeDtypeStruct(shapes[1], jnp.bfloat16),
        ),
        in_specs=[
            pl.BlockSpec(memory_space=pltpu.SMEM),
            pl.BlockSpec((1, row_list), lambda s: (0, 0)),
        ]
        + [pl.BlockSpec((part.shape[0], LANES), lambda s: (0, tail)) for part in rest],
        out_specs=[pl.BlockSpec(shape, lambda s: (0, 0)) for shape in shapes],
        compiler_params=params(16),
        name="tables",
    )(doc_lengths, dest, *rest)


def attend_kernel(n_keys, n_out, ids, q_ref, q_new, bias, chosen, *refs):
    kv_refs = refs[:n_keys]
    outs = refs[-1 - n_out : -1]
    q_all = refs[-1]
    row_list = q_ref.shape[0]
    capacity = outs[0].shape[0]

    q_all[...] = q_ref[...]
    for part in range(NSWAP):
        at = pl.multiple_of(ids[0, 0, part] * BLK, BLK)
        q_all[pl.ds(at, BLK), :] = q_new[part * BLK : (part + 1) * BLK, :]

    for j in range(PER_STEP):
        wide = PORTION * HEAD_SIZE
        at = slice(j * 2 * HEAD_SIZE, (j + 1) * 2 * HEAD_SIZE)
        key = jnp.concatenate([ref[:, at.start : at.start + HEAD_SIZE] for ref in kv_refs], axis=0)
        value = jnp.concatenate([ref[:, at.start + HEAD_SIZE : at.stop] for ref in kv_refs], axis=0)
        first = j * PORTION
        query = jnp.concatenate(
            [
                q_all[:, (first + h) * HEAD_SIZE : (first + h + 1) * HEAD_SIZE]
                for h in range(PORTION)
            ],
            axis=0,
        )
        scores = lax.dot_general(
            query, key, (((1,), (1,)), ((), ())), preferred_element_type=jnp.float32
        )
        scores = scores + jnp.concatenate([bias[...]] * PORTION, axis=0)
        top = jnp.max(scores, axis=1, keepdims=True)
        expo = jnp.exp2((scores - top) * (math.log2(math.e) / math.sqrt(HEAD_SIZE)))
        total = jnp.sum(expo, axis=1, keepdims=True)
        attn = jnp.dot(expo.astype(jnp.bfloat16), value, preferred_element_type=jnp.float32)
        attn = (attn / total).astype(jnp.bfloat16)
        attn = jnp.concatenate(
            [attn[h * row_list : (h + 1) * row_list] for h in range(PORTION)], axis=1
        )
        routed = jnp.dot(chosen[...], attn, preferred_element_type=jnp.float32).astype(jnp.bfloat16)
        for k in range(n_out):
            outs[k][:, j * wide : (j + 1) * wide] = routed[k * capacity : (k + 1) * capacity]


def attend(first, heads, swap_ids, queries, q_new, bias, chosen, kv_parts, before):
    row_list, n_all = bias.shape
    n_out = lax.axis_size("inner")
    capacity = NSWAP * row_list // n_out
    wide = PORTION * HEAD_SIZE

    def columns(rows, width):
        return pl.BlockSpec((rows, width), lambda s: (0, first // PER_STEP + s))

    def whole(array):
        return pl.BlockSpec(array.shape, lambda s: (0, 0))

    return pl.pallas_call(
        functools.partial(attend_kernel, len(kv_parts), n_out),
        grid=(heads // PER_STEP,),
        out_shape=[jax.ShapeDtypeStruct((capacity, heads * wide), jnp.bfloat16)] * n_out,
        in_specs=[
            pl.BlockSpec(memory_space=pltpu.SMEM),
            columns(row_list, PER_STEP * wide),
            columns(NSWAP * BLK, PER_STEP * wide),
            whole(bias),
            whole(chosen),
        ]
        + [columns(part.shape[0], PER_STEP * 2 * HEAD_SIZE) for part in kv_parts]
        + [pl.BlockSpec(memory_space=pl.ANY)] * len(before),
        out_specs=[pl.BlockSpec((capacity, PER_STEP * wide), lambda s: (0, s))] * n_out,
        scratch_shapes=[pltpu.VMEM((row_list, PER_STEP * wide), jnp.bfloat16)],
        compiler_params=params(16 if before else 60),
        cost_estimate=pl.CostEstimate(
            flops=heads * PORTION * row_list * n_all * HEAD_SIZE * 4,
            bytes_accessed=heads * (4 * wide * row_list * 2 + n_all * 512),
            transcendentals=heads * PORTION * row_list * n_all,
        ),
        name="attend",
    )(swap_ids, queries, q_new, bias, chosen, *kv_parts, *before)


def squares_kernel(*refs):
    n_parts = len(refs) // 2
    for ref, out in zip(refs[:n_parts], refs[n_parts:]):
        value = ref[...].astype(jnp.float32)
        out[...] = jnp.broadcast_to(jnp.sum(value * value, axis=1, keepdims=True), out.shape)


def squares(parts):
    capacity, wide = parts[0].shape
    return pl.pallas_call(
        squares_kernel,
        out_shape=[jax.ShapeDtypeStruct((capacity, LANES), jnp.float32)] * len(parts),
        compiler_params=params(16),
        cost_estimate=pl.CostEstimate(
            flops=PLACE_EARLY,
            bytes_accessed=len(parts) * capacity * wide * 2,
            transcendentals=0,
        ),
        name="squares",
    )(*parts)


def norm_kernel(me, gain, early, first, others, *refs):
    out = refs[-1]
    first, others = first[...].astype(jnp.float32), others[...].astype(jnp.float32)
    cut, width = first.shape[1], out.shape[1]
    total = early[...][:, :1] + jnp.sum(others * others, axis=1, keepdims=True)
    factor = lax.rsqrt(total / width + 1e-06)
    out[:, :cut] = (first * factor * gain[:, :cut]).astype(jnp.bfloat16)
    out[:, cut:] = (others * factor * gain[:, cut:]).astype(jnp.bfloat16)


def normalize(source, gain, early, first, others, n_inner, result):
    capacity, cut = first.shape
    width = gain.shape[0]
    steps = 2
    rows = capacity // steps
    held = [] if result is None else [result]
    return pl.pallas_call(
        norm_kernel,
        out_shape=jax.ShapeDtypeStruct((n_inner * capacity, width), jnp.bfloat16),
        grid_spec=pltpu.PrefetchScalarGridSpec(
            num_scalar_prefetch=1,
            grid=(steps,),
            in_specs=[
                pl.BlockSpec((1, width), lambda s, at: (0, 0)),
                pl.BlockSpec((rows, LANES), lambda s, at: (s, 0)),
                pl.BlockSpec((rows, cut), lambda s, at: (s, 0)),
                pl.BlockSpec((rows, width - cut), lambda s, at: (s, 0)),
            ]
            + [pl.BlockSpec(memory_space=pl.ANY)] * len(held),
            out_specs=pl.BlockSpec((rows, width), lambda s, at: (at[0] * steps + s, 0)),
        ),
        input_output_aliases={5: 0} if held else {},
        compiler_params=params(16),
        name="normalize",
    )(source.reshape(1), gain.reshape(1, width), early, first, others, *held)


def shards(queries, key_values, doc_lengths, pairing, swap_ids, dest, gain):
    n_inner = lax.axis_size("inner")
    n_outer = lax.axis_size("outer")
    me = lax.axis_index("inner")
    n_back = n_inner // 2

    kv_rest, kv_listed, q_listed = split_blocks(swap_ids, queries, key_values)
    branches = [
        functools.partial(gather_keys, mask, n_outer, n_inner, n_back)
        for mask in range(1, n_outer)
    ]
    q_new, rest, listed, bias, chosen = lax.switch(
        pairing[0] - 1, branches, doc_lengths, dest.reshape(1, -1), kv_rest, kv_listed, q_listed
    )
    kv_parts = [part for pair in zip([kv_rest] + rest, listed) for part in pair]

    arrived, first, before = [], 0, []
    for heads in HEAD_GROUPS:
        routed = attend(
            first, heads, swap_ids, queries, q_new, bias, chosen, kv_parts, before
        )
        before = [routed[0]]
        arrived.append(routed[0])
        for k in range(1, n_inner):
            arrived.append(lax.ppermute(routed[k], "inner", ring(k, n_inner)))
        first += heads
    early = squares(arrived[:n_inner])
    result = None
    for k in range(n_inner):
        source = lax.rem(me - k + n_inner, n_inner)
        result = normalize(
            source, gain, early[k], arrived[k], arrived[n_inner + k], n_inner, result
        )
    return result


def solution(mesh):
    return jax.shard_map(
        shards,
        mesh=mesh,
        in_specs=(
            P(("outer", "inner"), None),
            P(("outer", "inner"), None),
            P("outer", None),
            P(),
            P("outer", "inner", None),
            P(("outer", "inner"), None),
            P(),
        ),
        out_specs=P(("outer", "inner"), None),
        check_vma=False,
    )
```

```python
import functools
import math

import jax
import jax.numpy as jnp
from jax import lax
from jax.experimental import pallas as pl
from jax.experimental.pallas import tpu as pltpu
from jax.sharding import PartitionSpec as P

QUERY_HEADS = 40
KEY_VALUE_HEADS = 8
PORTION = QUERY_HEADS // KEY_VALUE_HEADS
HEAD_SIZE = 128
BLK = 32
NSWAP = 2
LANES = 128

NEGATIVE_LARGE = -1e30
HEAD_GROUPS = (2, 6)
PLACE_EARLY = 30_000_000_000
PER_STEP = 2
MIB = 1024 * 1024


def params(mib=60):
    return pltpu.CompilerParams(vmem_limit_bytes=mib * MIB)


def ring(step, size):
    return [(i, (i + step) % size) for i in range(size)]


def block_order(listed, n_blocks):
    low, high = listed
    first = jnp.where(low > 0, 0, jnp.where(high > 1, 1, 2))
    return [first, n_blocks * (n_blocks - 1) // 2 - first - low - high, low, high]


def split_kernel(ids, q_ref, kv_ref, kv_rest, kv_listed, q_listed, sems):
    n_blocks = kv_ref.shape[0] // BLK
    n_rest = n_blocks - NSWAP
    kv_width = kv_ref.shape[1]
    order = block_order((ids[0, 0, 0], ids[0, 0, 1]), n_blocks)
    copies = []
    for b, block in enumerate(order):
        here = pl.ds(pl.multiple_of(block * BLK, BLK), BLK)
        there = pl.ds(b % n_rest * BLK, BLK)
        if b < n_rest:
            pairs = [(kv_ref, kv_rest.at[there, pl.ds(0, kv_width)])]
        else:
            pairs = [(kv_ref, kv_listed.at[there]), (q_ref, q_listed.at[there])]
        for source, target in pairs:
            copies.append(pltpu.make_async_copy(source.at[here], target, sems.at[len(copies)]))
            copies[-1].start()
    shape = (kv_rest.shape[0], LANES)
    row = lax.broadcasted_iota(jnp.int32, shape, 0)
    lane = lax.broadcasted_iota(jnp.int32, shape, 1)
    pos = jnp.zeros(shape, jnp.int32)
    for b, block in enumerate(order):
        at = b % n_rest * BLK
        here = (row >= at) & (row < at + BLK) & (lane == b // n_rest)
        pos = jnp.where(here, row - at + block * BLK, pos)
    kv_rest[:, kv_width:] = pos.astype(jnp.bfloat16)
    for copy in copies:
        copy.wait()


def split_blocks(swap_ids, queries, key_values):
    row_list, width = queries.shape
    kv_width = key_values.shape[1]
    some = NSWAP * BLK
    far = pl.BlockSpec(memory_space=pltpu.HBM)
    near = pl.BlockSpec(memory_space=pltpu.VMEM)
    return pl.pallas_call(
        split_kernel,
        out_shape=(
            pltpu.VMEM((row_list - some, kv_width + LANES), jnp.bfloat16),
            pltpu.VMEM((some, kv_width), jnp.bfloat16),
            pltpu.VMEM((some, width), jnp.bfloat16),
        ),
        in_specs=[pl.BlockSpec(memory_space=pltpu.SMEM), far, far],
        out_specs=(near,) * 3,
        scratch_shapes=[pltpu.SemaphoreType.DMA((row_list // BLK + NSWAP,))],
        compiler_params=params(16),
        name="split_blocks",
    )(
        pltpu.with_memory_space_constraint(swap_ids, pltpu.HBM),
        pltpu.with_memory_space_constraint(queries, pltpu.HBM),
        pltpu.with_memory_space_constraint(key_values, pltpu.HBM),
    )


def back(value, n_inner, step):
    pairs = ring(1, n_inner) if step == 1 else [(i, i + 1) for i in range(step - 1, n_inner - 1)]
    return lax.ppermute(value, "inner", pairs)


def gather_keys(mask, n_outer, n_inner, n_back, doc_lengths, dest, kv_rest, kv_listed, q_listed):
    def cross(value, bits):
        return lax.ppermute(value, "outer", [(i, i ^ bits) for i in range(n_outer)])

    def swap(value):
        if mask & 1 and mask > 1:
            return cross(cross(value, 1), mask - 1)
        return cross(value, mask)

    def reach_back(value, whole_ring):
        parts = [value]
        for _ in range(n_back):
            parts.append(back(parts[-1], n_inner, 1 if whole_ring else len(parts)))
        return parts

    rest = reach_back(kv_rest, True)
    listed = reach_back(swap(kv_listed), False)
    row_list = dest.shape[1]
    n_all = (n_back + 1) * row_list
    bias, chosen = tables(doc_lengths, dest, rest, row_list, n_all, n_inner)
    return swap(q_listed), rest[1:], listed, bias, chosen


def fill_tables(n_out, lengths, dest, pos_refs, bias, chosen):
    row_list, n_all = bias.shape
    me = lax.axis_index("inner")
    lane = lax.broadcasted_iota(jnp.int32, (1, LANES), 1)
    key_pos = []
    for back, ref in enumerate(pos_refs):
        for which in range(2):
            pick = (lane == which).astype(jnp.bfloat16)
            pos = lax.dot_general(
                pick, ref[...], (((1,), (1,)), ((), ())), preferred_element_type=jnp.float32
            ).astype(jnp.int32)
            key_pos.append(jnp.where(me >= back, pos + (me - back) * row_list, -1))
    key_pos = jnp.concatenate(key_pos, axis=1)
    q_pos = me * row_list + lax.broadcasted_iota(jnp.int32, (row_list, 1), 0)
    end, start = 0, jnp.zeros((row_list, 1), jnp.int32)
    for k in range(lengths.shape[1]):
        end = end + lengths[0, k]
        start = jnp.where(q_pos >= end, end, start)
    bias[...] = jnp.where((key_pos <= q_pos) & (key_pos >= start), 0.0, NEGATIVE_LARGE)

    capacity = chosen.shape[0] // n_out
    square = (row_list, row_list)
    named = lax.broadcasted_iota(jnp.int32, square, 0) == dest[...]
    earlier = lax.broadcasted_iota(jnp.int32, square, 0) < lax.broadcasted_iota(jnp.int32, square, 1)
    before = jnp.dot(
        named.astype(jnp.bfloat16), earlier.astype(jnp.bfloat16), preferred_element_type=jnp.float32
    )
    rank = jnp.sum(jnp.where(named, before, 0.0), axis=0, keepdims=True).astype(jnp.int32)
    place = lax.rem(dest[...] - me + n_out, n_out) * capacity + rank
    slots = lax.broadcasted_iota(jnp.int32, chosen.shape, 0)
    chosen[...] = (slots == place).astype(jnp.bfloat16)


def tables_kernel(n_ranges, n_out, lengths, dest, *refs):
    fill_tables(n_out, lengths, dest, refs[:n_ranges], *refs[n_ranges:])


def tables(doc_lengths, dest, rest, row_list, n_all, n_out):
    capacity = NSWAP * row_list // n_out
    tail = rest[0].shape[1] // LANES - 1
    shapes = ((row_list, n_all), (n_out * capacity, row_list))
    return pl.pallas_call(
        functools.partial(tables_kernel, len(rest), n_out),
        grid=(1,),
        out_shape=(
            jax.ShapeDtypeStruct(shapes[0], jnp.float32),
            jax.ShapeDtypeStruct(shapes[1], jnp.bfloat16),
        ),
        in_specs=[
            pl.BlockSpec(memory_space=pltpu.SMEM),
            pl.BlockSpec((1, row_list), lambda s: (0, 0)),
        ]
        + [pl.BlockSpec((part.shape[0], LANES), lambda s: (0, tail)) for part in rest],
        out_specs=[pl.BlockSpec(shape, lambda s: (0, 0)) for shape in shapes],
        compiler_params=params(16),
        name="tables",
    )(doc_lengths, dest, *rest)


def attend_kernel(n_keys, n_out, ids, q_ref, q_new, bias, chosen, *refs):
    kv_refs = refs[:n_keys]
    outs = refs[-1 - n_out : -1]
    q_all = refs[-1]
    row_list = q_ref.shape[0]
    capacity = outs[0].shape[0]

    q_all[...] = q_ref[...]
    for part in range(NSWAP):
        at = pl.multiple_of(ids[0, 0, part] * BLK, BLK)
        q_all[pl.ds(at, BLK), :] = q_new[part * BLK : (part + 1) * BLK, :]

    for j in range(PER_STEP):
        wide = PORTION * HEAD_SIZE
        at = slice(j * 2 * HEAD_SIZE, (j + 1) * 2 * HEAD_SIZE)
        key = jnp.concatenate([ref[:, at.start : at.start + HEAD_SIZE] for ref in kv_refs], axis=0)
        value = jnp.concatenate([ref[:, at.start + HEAD_SIZE : at.stop] for ref in kv_refs], axis=0)
        first = j * PORTION
        query = jnp.concatenate(
            [
                q_all[:, (first + h) * HEAD_SIZE : (first + h + 1) * HEAD_SIZE]
                for h in range(PORTION)
            ],
            axis=0,
        )
        scores = lax.dot_general(
            query, key, (((1,), (1,)), ((), ())), preferred_element_type=jnp.float32
        )
        scores = scores + jnp.concatenate([bias[...]] * PORTION, axis=0)
        top = jnp.max(scores, axis=1, keepdims=True)
        expo = jnp.exp2((scores - top) * (math.log2(math.e) / math.sqrt(HEAD_SIZE)))
        total = jnp.sum(expo, axis=1, keepdims=True)
        attn = jnp.dot(expo.astype(jnp.bfloat16), value, preferred_element_type=jnp.float32)
        attn = (attn / total).astype(jnp.bfloat16)
        attn = jnp.concatenate(
            [attn[h * row_list : (h + 1) * row_list] for h in range(PORTION)], axis=1
        )
        routed = jnp.dot(chosen[...], attn, preferred_element_type=jnp.float32).astype(jnp.bfloat16)
        for k in range(n_out):
            outs[k][:, j * wide : (j + 1) * wide] = routed[k * capacity : (k + 1) * capacity]


def attend(first, heads, swap_ids, queries, q_new, bias, chosen, kv_parts, before):
    row_list, n_all = bias.shape
    n_out = lax.axis_size("inner")
    capacity = NSWAP * row_list // n_out
    wide = PORTION * HEAD_SIZE

    def columns(rows, width):
        return pl.BlockSpec((rows, width), lambda s: (0, first // PER_STEP + s))

    def whole(array):
        return pl.BlockSpec(array.shape, lambda s: (0, 0))

    return pl.pallas_call(
        functools.partial(attend_kernel, len(kv_parts), n_out),
        grid=(heads // PER_STEP,),
        out_shape=[jax.ShapeDtypeStruct((capacity, heads * wide), jnp.bfloat16)] * n_out,
        in_specs=[
            pl.BlockSpec(memory_space=pltpu.SMEM),
            columns(row_list, PER_STEP * wide),
            columns(NSWAP * BLK, PER_STEP * wide),
            whole(bias),
            whole(chosen),
        ]
        + [columns(part.shape[0], PER_STEP * 2 * HEAD_SIZE) for part in kv_parts]
        + [pl.BlockSpec(memory_space=pl.ANY)] * len(before),
        out_specs=[pl.BlockSpec((capacity, PER_STEP * wide), lambda s: (0, s))] * n_out,
        scratch_shapes=[pltpu.VMEM((row_list, PER_STEP * wide), jnp.bfloat16)],
        compiler_params=params(16 if before else 60),
        cost_estimate=pl.CostEstimate(
            flops=heads * PORTION * row_list * n_all * HEAD_SIZE * 4,
            bytes_accessed=heads * (4 * wide * row_list * 2 + n_all * 512),
            transcendentals=heads * PORTION * row_list * n_all,
        ),
        name="attend",
    )(swap_ids, queries, q_new, bias, chosen, *kv_parts, *before)


def squares_kernel(*refs):
    n_parts = len(refs) // 2
    for ref, out in zip(refs[:n_parts], refs[n_parts:]):
        value = ref[...].astype(jnp.float32)
        out[...] = jnp.broadcast_to(jnp.sum(value * value, axis=1, keepdims=True), out.shape)


def squares(parts):
    capacity, wide = parts[0].shape
    return pl.pallas_call(
        squares_kernel,
        out_shape=[jax.ShapeDtypeStruct((capacity, LANES), jnp.float32)] * len(parts),
        compiler_params=params(16),
        cost_estimate=pl.CostEstimate(
            flops=PLACE_EARLY,
            bytes_accessed=len(parts) * capacity * wide * 2,
            transcendentals=0,
        ),
        name="squares",
    )(*parts)


def norm_kernel(me, gain, early, first, others, *refs):
    out = refs[-1]
    first, others = first[...].astype(jnp.float32), others[...].astype(jnp.float32)
    cut, width = first.shape[1], out.shape[1]
    total = early[...][:, :1] + jnp.sum(others * others, axis=1, keepdims=True)
    factor = lax.rsqrt(total / width + 1e-06)
    out[:, :cut] = (first * factor * gain[:, :cut]).astype(jnp.bfloat16)
    out[:, cut:] = (others * factor * gain[:, cut:]).astype(jnp.bfloat16)


def normalize(source, gain, early, first, others, n_inner, result):
    capacity, cut = first.shape
    width = gain.shape[0]
    steps = 2
    rows = capacity // steps
    held = [] if result is None else [result]
    return pl.pallas_call(
        norm_kernel,
        out_shape=jax.ShapeDtypeStruct((n_inner * capacity, width), jnp.bfloat16),
        grid_spec=pltpu.PrefetchScalarGridSpec(
            num_scalar_prefetch=1,
            grid=(steps,),
            in_specs=[
                pl.BlockSpec((1, width), lambda s, at: (0, 0)),
                pl.BlockSpec((rows, LANES), lambda s, at: (s, 0)),
                pl.BlockSpec((rows, cut), lambda s, at: (s, 0)),
                pl.BlockSpec((rows, width - cut), lambda s, at: (s, 0)),
            ]
            + [pl.BlockSpec(memory_space=pl.ANY)] * len(held),
            out_specs=pl.BlockSpec((rows, width), lambda s, at: (at[0] * steps + s, 0)),
        ),
        input_output_aliases={5: 0} if held else {},
        compiler_params=params(16),
        name="normalize",
    )(source.reshape(1), gain.reshape(1, width), early, first, others, *held)


def shards(queries, key_values, doc_lengths, pairing, swap_ids, dest, gain):
    n_inner = lax.axis_size("inner")
    n_outer = lax.axis_size("outer")
    me = lax.axis_index("inner")
    n_back = n_inner // 2

    kv_rest, kv_listed, q_listed = split_blocks(swap_ids, queries, key_values)
    branches = [
        functools.partial(gather_keys, mask, n_outer, n_inner, n_back)
        for mask in range(1, n_outer)
    ]
    q_new, rest, listed, bias, chosen = lax.switch(
        pairing[0] - 1, branches, doc_lengths, dest.reshape(1, -1), kv_rest, kv_listed, q_listed
    )
    kv_parts = [part for pair in zip([kv_rest] + rest, listed) for part in pair]

    arrived, first, before = [], 0, []
    for heads in HEAD_GROUPS:
        routed = attend(
            first, heads, swap_ids, queries, q_new, bias, chosen, kv_parts, before
        )
        before = [routed[0]]
        arrived.append(routed[0])
        for k in range(1, n_inner):
            arrived.append(lax.ppermute(routed[k], "inner", ring(k, n_inner)))
        first += heads
    early = squares(arrived[:n_inner])
    result = None
    for k in range(n_inner):
        source = lax.rem(me - k + n_inner, n_inner)
        result = normalize(
            source, gain, early[k], arrived[k], arrived[n_inner + k], n_inner, result
        )
    return result


def solution(mesh):
    return jax.shard_map(
        shards,
        mesh=mesh,
        in_specs=(
            P(("outer", "inner"), None),
            P(("outer", "inner"), None),
            P("outer", None),
            P(),
            P("outer", "inner", None),
            P(("outer", "inner"), None),
            P(),
        ),
        out_specs=P(("outer", "inner"), None),
        check_vma=False,
    )
```

```python
import functools
import math

import jax
import jax.numpy as jnp
from jax import lax
from jax.experimental import pallas as pl
from jax.experimental.pallas import tpu as pltpu
from jax.sharding import PartitionSpec as P

QUERY_HEADS = 40
KEY_VALUE_HEADS = 8
PORTION = QUERY_HEADS // KEY_VALUE_HEADS
HEAD_SIZE = 128
BLK = 32
NSWAP = 2
LANES = 128

NEGATIVE_LARGE = -1e30
HEAD_GROUPS = (2, 6)
PLACE_EARLY = 30_000_000_000
PER_STEP = 2
MIB = 1024 * 1024


def params(mib=60):
    return pltpu.CompilerParams(vmem_limit_bytes=mib * MIB)


def ring(step, size):
    return [(i, (i + step) % size) for i in range(size)]


def block_order(listed, n_blocks):
    low, high = listed
    first = jnp.where(low > 0, 0, jnp.where(high > 1, 1, 2))
    return [first, n_blocks * (n_blocks - 1) // 2 - first - low - high, low, high]


def split_kernel(ids, q_ref, kv_ref, kv_rest, kv_listed, q_listed, sems):
    n_blocks = kv_ref.shape[0] // BLK
    n_rest = n_blocks - NSWAP
    kv_width = kv_ref.shape[1]
    order = block_order((ids[0, 0, 0], ids[0, 0, 1]), n_blocks)
    copies = []
    for b, block in enumerate(order):
        here = pl.ds(pl.multiple_of(block * BLK, BLK), BLK)
        there = pl.ds(b % n_rest * BLK, BLK)
        if b < n_rest:
            pairs = [(kv_ref, kv_rest.at[there, pl.ds(0, kv_width)])]
        else:
            pairs = [(kv_ref, kv_listed.at[there]), (q_ref, q_listed.at[there])]
        for source, target in pairs:
            copies.append(pltpu.make_async_copy(source.at[here], target, sems.at[len(copies)]))
            copies[-1].start()
    shape = (kv_rest.shape[0], LANES)
    row = lax.broadcasted_iota(jnp.int32, shape, 0)
    lane = lax.broadcasted_iota(jnp.int32, shape, 1)
    pos = jnp.zeros(shape, jnp.int32)
    for b, block in enumerate(order):
        at = b % n_rest * BLK
        here = (row >= at) & (row < at + BLK) & (lane == b // n_rest)
        pos = jnp.where(here, row - at + block * BLK, pos)
    kv_rest[:, kv_width:] = pos.astype(jnp.bfloat16)
    for copy in copies:
        copy.wait()


def split_blocks(swap_ids, queries, key_values):
    row_list, width = queries.shape
    kv_width = key_values.shape[1]
    some = NSWAP * BLK
    far = pl.BlockSpec(memory_space=pltpu.HBM)
    near = pl.BlockSpec(memory_space=pltpu.VMEM)
    return pl.pallas_call(
        split_kernel,
        out_shape=(
            pltpu.VMEM((row_list - some, kv_width + LANES), jnp.bfloat16),
            pltpu.VMEM((some, kv_width), jnp.bfloat16),
            pltpu.VMEM((some, width), jnp.bfloat16),
        ),
        in_specs=[pl.BlockSpec(memory_space=pltpu.SMEM), far, far],
        out_specs=(near,) * 3,
        scratch_shapes=[pltpu.SemaphoreType.DMA((row_list // BLK + NSWAP,))],
        compiler_params=params(16),
        name="split_blocks",
    )(
        pltpu.with_memory_space_constraint(swap_ids, pltpu.HBM),
        pltpu.with_memory_space_constraint(queries, pltpu.HBM),
        pltpu.with_memory_space_constraint(key_values, pltpu.HBM),
    )


def back(value, n_inner, step):
    pairs = ring(1, n_inner) if step == 0 else [(i, i + 1) for i in range(step - 1, n_inner - 1)]
    return lax.ppermute(value, "inner", pairs)


def gather_keys(mask, n_outer, n_inner, n_back, doc_lengths, dest, kv_rest, kv_listed, q_listed):
    def cross(value, bits):
        return lax.ppermute(value, "outer", [(i, i ^ bits) for i in range(n_outer)])

    def swap(value):
        if mask & 1 and mask > 1:
            return cross(cross(value, 1), mask - 1)
        return cross(value, mask)

    def reach_back(value, whole_ring):
        parts = [value]
        for _ in range(n_back):
            parts.append(back(parts[-1], n_inner, 0 if whole_ring else len(parts)))
        return parts

    rest = reach_back(kv_rest, True)
    listed = reach_back(swap(kv_listed), False)
    row_list = dest.shape[1]
    n_all = (n_back + 1) * row_list
    bias, chosen = tables(doc_lengths, dest, rest, row_list, n_all, n_inner)
    return swap(q_listed), rest[1:], listed, bias, chosen


def fill_tables(n_out, lengths, dest, pos_refs, bias, chosen):
    row_list, n_all = bias.shape
    me = lax.axis_index("inner")
    lane = lax.broadcasted_iota(jnp.int32, (1, LANES), 1)
    key_pos = []
    for back, ref in enumerate(pos_refs):
        for which in range(2):
            pick = (lane == which).astype(jnp.bfloat16)
            pos = lax.dot_general(
                pick, ref[...], (((1,), (1,)), ((), ())), preferred_element_type=jnp.float32
            ).astype(jnp.int32)
            key_pos.append(jnp.where(me >= back, pos + (me - back) * row_list, -1))
    key_pos = jnp.concatenate(key_pos, axis=1)
    q_pos = me * row_list + lax.broadcasted_iota(jnp.int32, (row_list, 1), 0)
    end, start = 0, jnp.zeros((row_list, 1), jnp.int32)
    for k in range(lengths.shape[1]):
        end = end + lengths[0, k]
        start = jnp.where(q_pos >= end, end, start)
    bias[...] = jnp.where((key_pos <= q_pos) & (key_pos >= start), 0.0, NEGATIVE_LARGE)

    capacity = chosen.shape[0] // n_out
    square = (row_list, row_list)
    named = lax.broadcasted_iota(jnp.int32, square, 0) == dest[...]
    earlier = lax.broadcasted_iota(jnp.int32, square, 0) < lax.broadcasted_iota(jnp.int32, square, 1)
    before = jnp.dot(
        named.astype(jnp.bfloat16), earlier.astype(jnp.bfloat16), preferred_element_type=jnp.float32
    )
    rank = jnp.sum(jnp.where(named, before, 0.0), axis=0, keepdims=True).astype(jnp.int32)
    place = lax.rem(dest[...] - me + n_out, n_out) * capacity + rank
    slots = lax.broadcasted_iota(jnp.int32, chosen.shape, 0)
    chosen[...] = (slots == place).astype(jnp.bfloat16)


def tables_kernel(n_ranges, n_out, lengths, dest, *refs):
    fill_tables(n_out, lengths, dest, refs[:n_ranges], *refs[n_ranges:])


def tables(doc_lengths, dest, rest, row_list, n_all, n_out):
    capacity = NSWAP * row_list // n_out
    tail = rest[0].shape[1] // LANES - 1
    shapes = ((row_list, n_all), (n_out * capacity, row_list))
    return pl.pallas_call(
        functools.partial(tables_kernel, len(rest), n_out),
        grid=(1,),
        out_shape=(
            jax.ShapeDtypeStruct(shapes[0], jnp.float32),
            jax.ShapeDtypeStruct(shapes[1], jnp.bfloat16),
        ),
        in_specs=[
            pl.BlockSpec(memory_space=pltpu.SMEM),
            pl.BlockSpec((1, row_list), lambda s: (0, 0)),
        ]
        + [pl.BlockSpec((part.shape[0], LANES), lambda s: (0, tail)) for part in rest],
        out_specs=[pl.BlockSpec(shape, lambda s: (0, 0)) for shape in shapes],
        compiler_params=params(16),
        name="tables",
    )(doc_lengths, dest, *rest)


def attend_kernel(n_keys, n_out, ids, q_ref, q_new, bias, chosen, *refs):
    kv_refs = refs[:n_keys]
    outs = refs[-1 - n_out : -1]
    q_all = refs[-1]
    row_list = q_ref.shape[0]
    capacity = outs[0].shape[0]

    q_all[...] = q_ref[...]
    for part in range(NSWAP):
        at = pl.multiple_of(ids[0, 0, part] * BLK, BLK)
        q_all[pl.ds(at, BLK), :] = q_new[part * BLK : (part + 1) * BLK, :]

    for j in range(PER_STEP):
        wide = PORTION * HEAD_SIZE
        at = slice(j * 2 * HEAD_SIZE, (j + 1) * 2 * HEAD_SIZE)
        key = jnp.concatenate([ref[:, at.start : at.start + HEAD_SIZE] for ref in kv_refs], axis=0)
        value = jnp.concatenate([ref[:, at.start + HEAD_SIZE : at.stop] for ref in kv_refs], axis=0)
        first = j * PORTION
        query = jnp.concatenate(
            [
                q_all[:, (first + h) * HEAD_SIZE : (first + h + 1) * HEAD_SIZE]
                for h in range(PORTION)
            ],
            axis=0,
        )
        scores = lax.dot_general(
            query, key, (((1,), (1,)), ((), ())), preferred_element_type=jnp.float32
        )
        scores = scores + jnp.concatenate([bias[...]] * PORTION, axis=0)
        top = jnp.max(scores, axis=1, keepdims=True)
        expo = jnp.exp2((scores - top) * (math.log2(math.e) / math.sqrt(HEAD_SIZE)))
        total = jnp.sum(expo, axis=1, keepdims=True)
        attn = jnp.dot(expo.astype(jnp.bfloat16), value, preferred_element_type=jnp.float32)
        attn = (attn / total).astype(jnp.bfloat16)
        attn = jnp.concatenate(
            [attn[h * row_list : (h + 1) * row_list] for h in range(PORTION)], axis=1
        )
        routed = jnp.dot(chosen[...], attn, preferred_element_type=jnp.float32).astype(jnp.bfloat16)
        for k in range(n_out):
            outs[k][:, j * wide : (j + 1) * wide] = routed[k * capacity : (k + 1) * capacity]


def attend(first, heads, swap_ids, queries, q_new, bias, chosen, kv_parts, before):
    row_list, n_all = bias.shape
    n_out = lax.axis_size("inner")
    capacity = NSWAP * row_list // n_out
    wide = PORTION * HEAD_SIZE

    def columns(rows, width):
        return pl.BlockSpec((rows, width), lambda s: (0, first // PER_STEP + s))

    def whole(array):
        return pl.BlockSpec(array.shape, lambda s: (0, 0))

    return pl.pallas_call(
        functools.partial(attend_kernel, len(kv_parts), n_out),
        grid=(heads // PER_STEP,),
        out_shape=[jax.ShapeDtypeStruct((capacity, heads * wide), jnp.bfloat16)] * n_out,
        in_specs=[
            pl.BlockSpec(memory_space=pltpu.SMEM),
            columns(row_list, PER_STEP * wide),
            columns(NSWAP * BLK, PER_STEP * wide),
            whole(bias),
            whole(chosen),
        ]
        + [columns(part.shape[0], PER_STEP * 2 * HEAD_SIZE) for part in kv_parts]
        + [pl.BlockSpec(memory_space=pl.ANY)] * len(before),
        out_specs=[pl.BlockSpec((capacity, PER_STEP * wide), lambda s: (0, s))] * n_out,
        scratch_shapes=[pltpu.VMEM((row_list, PER_STEP * wide), jnp.bfloat16)],
        compiler_params=params(16 if before else 60),
        cost_estimate=pl.CostEstimate(
            flops=heads * PORTION * row_list * n_all * HEAD_SIZE * 4,
            bytes_accessed=heads * (4 * wide * row_list * 2 + n_all * 512),
            transcendentals=heads * PORTION * row_list * n_all,
        ),
        name="attend",
    )(swap_ids, queries, q_new, bias, chosen, *kv_parts, *before)


def squares_kernel(*refs):
    n_parts = len(refs) // 2
    for ref, out in zip(refs[:n_parts], refs[n_parts:]):
        value = ref[...].astype(jnp.float32)
        out[...] = jnp.broadcast_to(jnp.sum(value * value, axis=1, keepdims=True), out.shape)


def squares(parts):
    capacity, wide = parts[0].shape
    return pl.pallas_call(
        squares_kernel,
        out_shape=[jax.ShapeDtypeStruct((capacity, LANES), jnp.float32)] * len(parts),
        compiler_params=params(16),
        cost_estimate=pl.CostEstimate(
            flops=PLACE_EARLY,
            bytes_accessed=len(parts) * capacity * wide * 2,
            transcendentals=0,
        ),
        name="squares",
    )(*parts)


def norm_kernel(me, gain, early, first, others, *refs):
    out = refs[-1]
    first, others = first[...].astype(jnp.float32), others[...].astype(jnp.float32)
    cut, width = first.shape[1], out.shape[1]
    total = early[...][:, :1] + jnp.sum(others * others, axis=1, keepdims=True)
    factor = lax.rsqrt(total / width + 1e-06)
    out[:, :cut] = (first * factor * gain[:, :cut]).astype(jnp.bfloat16)
    out[:, cut:] = (others * factor * gain[:, cut:]).astype(jnp.bfloat16)


def normalize(source, gain, early, first, others, n_inner, result):
    capacity, cut = first.shape
    width = gain.shape[0]
    steps = 2
    rows = capacity // steps
    held = [] if result is None else [result]
    return pl.pallas_call(
        norm_kernel,
        out_shape=jax.ShapeDtypeStruct((n_inner * capacity, width), jnp.bfloat16),
        grid_spec=pltpu.PrefetchScalarGridSpec(
            num_scalar_prefetch=1,
            grid=(steps,),
            in_specs=[
                pl.BlockSpec((1, width), lambda s, at: (0, 0)),
                pl.BlockSpec((rows, LANES), lambda s, at: (s, 0)),
                pl.BlockSpec((rows, cut), lambda s, at: (s, 0)),
                pl.BlockSpec((rows, width - cut), lambda s, at: (s, 0)),
            ]
            + [pl.BlockSpec(memory_space=pl.ANY)] * len(held),
            out_specs=pl.BlockSpec((rows, width), lambda s, at: (at[0] * steps + s, 0)),
        ),
        input_output_aliases={5: 0} if held else {},
        compiler_params=params(16),
        name="normalize",
    )(source.reshape(1), gain.reshape(1, width), early, first, others, *held)


def shards(queries, key_values, doc_lengths, pairing, swap_ids, dest, gain):
    n_inner = lax.axis_size("inner")
    n_outer = lax.axis_size("outer")
    me = lax.axis_index("inner")
    n_back = n_inner // 2

    kv_rest, kv_listed, q_listed = split_blocks(swap_ids, queries, key_values)
    branches = [
        functools.partial(gather_keys, mask, n_outer, n_inner, n_back)
        for mask in range(1, n_outer)
    ]
    q_new, rest, listed, bias, chosen = lax.switch(
        pairing[0] - 1, branches, doc_lengths, dest.reshape(1, -1), kv_rest, kv_listed, q_listed
    )
    kv_parts = [part for pair in zip([kv_rest] + rest, listed) for part in pair]

    arrived, first, before = [], 0, []
    for heads in HEAD_GROUPS:
        routed = attend(
            first, heads, swap_ids, queries, q_new, bias, chosen, kv_parts, before
        )
        before = [routed[0]]
        arrived.append(routed[0])
        for k in range(1, n_inner):
            arrived.append(lax.ppermute(routed[k], "inner", ring(k, n_inner)))
        first += heads
    early = squares(arrived[:n_inner])
    result = None
    for k in range(n_inner):
        source = lax.rem(me - k + n_inner, n_inner)
        result = normalize(
            source, gain, early[k], arrived[k], arrived[n_inner + k], n_inner, result
        )
    return result


def solution(mesh):
    return jax.shard_map(
        shards,
        mesh=mesh,
        in_specs=(
            P(("outer", "inner"), None),
            P(("outer", "inner"), None),
            P("outer", None),
            P(),
            P("outer", "inner", None),
            P(("outer", "inner"), None),
            P(),
        ),
        out_specs=P(("outer", "inner"), None),
        check_vma=False,
    )
```
